512 devices in a mesh: row: 16 (over y, z_hi, core), col: 32 (over z_lo, x).
Axes of the slice: x: 4, y: 4, z: 16 (z_hi: 2, z_lo: 8; z = z_hi * 8 + z_lo), core: 2. Of those that a mesh axis runs over, the one named last changes fastest.
Arguments:
- acts: bfloat16 [1024, 12288], P('col', 'row'), may hold values from -6 to 6
- weight: bfloat16 [12288, 24576], P('row', 'col'), may hold values from -0.0546875 to 0.0546875
- cotangent: bfloat16 [1024, 24576], P('row', 'col'), may hold values from -6 to 6
Outputs:
- output: bfloat16 [1024, 24576], P('row', 'col')
- acts_grad: bfloat16 [1024, 12288], P('col', 'row')
- weight_grad: bfloat16 [12288, 24576], P('row', 'col')
The draws below stay inside these ranges and needn't reach their ends.
All inputs are finite; a program needn't handle non-finite values.
Results may differ from the reference program's by a relative error of at most 0.0049.
Values may be sent and summed in bfloat16 or wider, within the bound.
No kernel may reach another device: no remote copies, remote signals or barrier semaphores. Data moves between devices by JAX's collectives and lax.ppermute only.
A program may use at most 64 MiB of HBM per device.

```python
import math
import jax
import jax.numpy as jnp
from jax import lax

D = 12288
FF = 24576
TOKENS = 1024


def levels(key, shape, pieces, low, high):
    gain, own = 1.0, jax.random.fold_in(key, 6)
    for position, blocks in pieces:
        heights = jnp.exp(jax.random.uniform(jax.random.fold_in(own, position), (blocks,), jnp.float32, low / len(pieces), high / len(pieces)))
        gain = gain * jnp.repeat(heights, shape[position] // blocks).reshape([-1 if axis == position else 1 for axis in range(len(shape))])
    return gain


def gaussian(key, dims, scale, bound, split=(), held_as=jnp.bfloat16):
    result = scale * jax.random.normal(key, dims, jnp.float32)
    if split:
        result = result * levels(key, dims, split, -0.22, 0.18)
    return jnp.clip(result, -bound, bound).astype(held_as)


def setup_inputs(seed: int = 0) -> dict:
    key_of = jax.random.split(jax.random.key(seed), 4)
    return {
        "acts": gaussian(key_of[0], (TOKENS, D), 1.0, 6.0, ((0, 32), (1, 16))),
        "weight": gaussian(key_of[1], (D, FF), D ** -0.5, 0.0546875, ((0, 16), (1, 32))),
        "cotangent": gaussian(key_of[2], (TOKENS, FF), 1.0, 6.0, ((0, 16), (1, 32))),
    }


def gelu_value(pre):
    return 0.5 * pre * (1.0 + lax.erf(pre / math.sqrt(2.0)))

def gelu_slope(pre):
    return 0.5 * (1.0 + lax.erf(pre / math.sqrt(2.0))) + pre * jnp.exp(-0.5 * pre * pre) / math.sqrt(2.0 * math.pi)

def reference(acts, weight, cotangent):
    pre = jnp.dot(acts, weight, preferred_element_type=jnp.float32)
    output = gelu_value(pre).astype(jnp.bfloat16)
    slope_grad = (cotangent.astype(jnp.float32) * gelu_slope(pre)).astype(jnp.bfloat16)
    acts_grad = jnp.dot(slope_grad, weight.T, preferred_element_type=jnp.float32).astype(jnp.bfloat16)
    weight_grad = (jnp.dot(acts.T, slope_grad, preferred_element_type=jnp.float32) * TOKENS ** (-0.5)).astype(jnp.bfloat16)
    return (output, acts_grad, weight_grad)
```

```python
import functools
import math

import jax
import jax.numpy as jnp
from jax import lax
from jax.experimental import pallas as pl
from jax.experimental.pallas import tpu as pltpu
from jax.sharding import PartitionSpec as P

ROWS, COLS = 16, 32
F32, BF16 = jnp.float32, jnp.bfloat16


def gelu_value(pre):
    return 0.5 * pre * (1.0 + lax.erf(pre / math.sqrt(2.0)))


def gelu_slope(pre):
    return 0.5 * (1.0 + lax.erf(pre / math.sqrt(2.0))) + pre * jnp.exp(
        -0.5 * pre * pre
    ) / math.sqrt(2.0 * math.pi)


def swap(value, axis, mask):
    size = ROWS if axis == "row" else COLS
    return lax.ppermute(value, axis, [(i, i ^ mask) for i in range(size)])


def row_place(block, me_row):
    rel = (block >> 1) ^ me_row
    y, zh, c = rel >> 2, (rel >> 1) & 1, rel & 1
    return ((c * 4 + y) * 2 + zh) * 2 + (block & 1)


def up_kernel(me, own, x1, x2, x3, w, send, keep, acts):
    me_row, me_col = me[0], me[1]
    part = own.shape[0] // 8
    for kx, piece in enumerate((own, x1, x2, x3)):
        for k in range(4):
            for j in range(2):
                block = me_col ^ (kx + 4 * k + 16 * j)
                to = pl.multiple_of(row_place(block, me_row) * part, part)
                acts[pl.ds(to, part), :] = piece[pl.ds((k * 2 + j) * part, part), :]
    half = acts.shape[0] // 2
    step = half // 2
    for i in range(2):
        rows = pl.ds(i * step, step)
        send[rows, :] = jnp.dot(
            acts[pl.ds(half + i * step, step), :], w[...], preferred_element_type=F32
        ).astype(BF16)
    for i in range(2):
        rows = pl.ds(i * step, step)
        keep[rows, :] = jnp.dot(acts[rows, :], w[...], preferred_element_type=F32)


def down_kernel(me, g0, g1, w, own, x1, x2, x3, held):
    me_row, me_col = me[0], me[1]
    part = own.shape[0] // 8
    for c, piece in enumerate((g0, g1)):
        for m in range(4):
            for h in range(2):
                rel = m * 4 + h * 2 + c
                for lo in range(2):
                    block = ((rel ^ me_row) * 2 + lo) ^ me_col
                    x, k, j = block & 3, (block >> 2) & 3, block >> 4
                    to = pl.multiple_of(((x * 4 + k) * 2 + j) * part, part)
                    held[pl.ds(to, part), :] = piece[
                        pl.ds(((m * 2 + h) * 2 + lo) * part, part), :
                    ]
    size = own.shape[0]
    for kx, out in ((2, x2), (1, x1), (3, x3), (0, own)):
        value = lax.dot_general(
            held[pl.ds(kx * size, size), :],
            w[...],
            (((1,), (1,)), ((), ())),
            preferred_element_type=F32,
        )
        out[...] = value.astype(out.dtype)


def call(kernel, outs, scratch, flops, *args):
    vmem = pl.BlockSpec(memory_space=pltpu.VMEM)
    return pl.pallas_call(
        kernel,
        out_shape=outs,
        in_specs=[pl.BlockSpec(memory_space=pltpu.SMEM)] + [vmem] * (len(args) - 1),
        out_specs=[vmem] * len(outs),
        scratch_shapes=scratch,
        compiler_params=pltpu.CompilerParams(vmem_limit_bytes=32 * 1024 * 1024),
        cost_estimate=pl.CostEstimate(
            flops=flops, bytes_accessed=6 * 1024 * 1024, transcendentals=0
        ),
    )(*args)


def shards(acts, weight, cotangent):
    me = jnp.stack([lax.axis_index("row"), lax.axis_index("col")]).astype(jnp.int32)
    part, depth = acts.shape
    width = weight.shape[1]
    tokens = part * COLS

    pair = jnp.concatenate([acts, swap(acts, "col", 16)])
    line = jnp.concatenate([pair] + [swap(pair, "col", 4 * k) for k in (1, 2, 3)])
    x2 = swap(line, "col", 2)
    x1 = swap(line, "col", 1)
    x3 = swap(line, "col", 3)

    flops = 2 * tokens * depth * width
    send, keep, acts_full = call(
        up_kernel,
        [
            jax.ShapeDtypeStruct((tokens // 2, width), BF16),
            jax.ShapeDtypeStruct((tokens // 2, width), F32),
            jax.ShapeDtypeStruct((tokens, depth), BF16),
        ],
        [],
        flops,
        me, line, x1, x2, x3, weight,
    )

    mine = keep + swap(send, "row", 1).astype(F32)
    size = tokens // 8
    sent = [mine[m * size : (m + 1) * size].astype(BF16) for m in (1, 2, 3)]
    got = [swap(s, "row", 4 * m) for s, m in zip(sent, (1, 2, 3))]
    mine = mine[:size] + got[0].astype(F32) + got[1].astype(F32) + got[2].astype(F32)
    size = tokens // 16
    pre = mine[:size] + swap(mine[size:].astype(BF16), "row", 2).astype(F32)

    output = gelu_value(pre).astype(BF16)
    grad = (cotangent.astype(F32) * gelu_slope(pre)).astype(BF16)

    pair = jnp.concatenate([grad, swap(grad, "row", 2)])
    g0 = jnp.concatenate([pair] + [swap(pair, "row", 4 * m) for m in (1, 2, 3)])
    g1 = swap(g0, "row", 1)

    size = tokens // 4
    mine, x1, x2, x3 = call(
        down_kernel,
        [jax.ShapeDtypeStruct((size, depth), F32)]
        + [jax.ShapeDtypeStruct((size, depth), BF16)] * 3,
        [pltpu.VMEM((tokens, width), BF16)],
        flops,
        me, g0, g1, weight,
    )

    x2 = swap(x2, "col", 2)
    x1 = swap(x1, "col", 1)
    x3 = swap(x3, "col", 3)
    mine = mine + x1.astype(F32) + x2.astype(F32) + x3.astype(F32)
    size = tokens // 16
    sent = [mine[k * size : (k + 1) * size].astype(BF16) for k in (1, 2, 3)]
    got = [swap(s, "col", 4 * k) for s, k in zip(sent, (1, 2, 3))]
    mine = mine[:size] + got[0].astype(F32) + got[1].astype(F32) + got[2].astype(F32)
    size = tokens // 32
    acts_grad = (
        mine[:size] + swap(mine[size:].astype(BF16), "col", 16).astype(F32)
    ).astype(BF16)

    grad_full = jnp.concatenate([g0, g1])
    weight_sum = lax.dot_general(
        acts_full, grad_full, (((0,), (0,)), ((), ())), preferred_element_type=F32
    )
    weight_grad = (weight_sum * tokens ** (-0.5)).astype(BF16)
    return (output, acts_grad, weight_grad)


def solution(mesh):
    in_specs = (P("col", "row"), P("row", "col"), P("row", "col"))
    out_specs = (P("row", "col"), P("col", "row"), P("row", "col"))
    return jax.shard_map(shards, mesh=mesh, in_specs=in_specs, out_specs=out_specs, check_vma=False)
```

```python
import functools
import math

import jax
import jax.numpy as jnp
from jax import lax
from jax.experimental import pallas as pl
from jax.experimental.pallas import tpu as pltpu
from jax.sharding import PartitionSpec as P

ROWS, COLS = 16, 32
CHUNKS = 1
F32, BF16 = jnp.float32, jnp.bfloat16
Y_GROUPS = [[y * 4 + low for y in range(4)] for low in range(4)]
X_GROUPS = [[z * 4 + x for x in range(4)] for z in range(8)]


def gelu_value(pre):
    return 0.5 * pre * (1.0 + lax.erf(pre / math.sqrt(2.0)))


def gelu_slope(pre):
    return 0.5 * (1.0 + lax.erf(pre / math.sqrt(2.0))) + pre * jnp.exp(
        -0.5 * pre * pre
    ) / math.sqrt(2.0 * math.pi)


def swap(value, axis, mask):
    size = ROWS if axis == "row" else COLS
    return lax.ppermute(value, axis, [(i, i ^ mask) for i in range(size)])


def spread(value, axis, groups):
    return lax.all_to_all(
        value, axis, split_axis=0, concat_axis=0, axis_index_groups=groups, tiled=True
    )


def row_place(block, me_row):
    owner = block >> 1
    return (((owner ^ me_row) & 1) * 8 + (owner >> 1)) * 2 + (block & 1)


def up_kernel(me, own, x1, x2, x3, w, _, send, keep, acts):
    me_row, me_col = me[0], me[1]
    part = own.shape[0] // 8
    for kx, piece in enumerate((own, x1, x2, x3)):
        for k in range(4):
            for j in range(2):
                block = me_col ^ (kx + 4 * k + 16 * j)
                to = pl.multiple_of(row_place(block, me_row) * part, part)
                acts[pl.ds(to, part), :] = piece[pl.ds((k * 2 + j) * part, part), :]
    half = acts.shape[0] // 2
    step = min(half, 256)
    for i in range(half // step):
        rows = pl.ds(i * step, step)
        send[rows, :] = jnp.dot(
            acts[pl.ds(half + i * step, step), :], w[...], preferred_element_type=F32
        ).astype(BF16)
    for i in range(half // step):
        rows = pl.ds(i * step, step)
        keep[rows, :] = jnp.dot(acts[rows, :], w[...], preferred_element_type=F32)


def down_kernel(me, g0, g1, w, out, held):
    me_row, me_col = me[0], me[1]
    part = g0.shape[0] // 16
    for c, piece in enumerate((g0, g1)):
        for yz in range(8):
            for lo in range(2):
                owner = yz * 2 + ((me_row & 1) ^ c)
                block = owner * 2 + lo
                rel = block ^ me_col
                x, k, j = block & 3, (rel >> 2) & 3, rel >> 4
                to = pl.multiple_of(((x * 4 + k) * 2 + j) * part, part)
                held[pl.ds(to, part), :] = piece[pl.ds((yz * 2 + lo) * part, part), :]
    step = 256
    for i in range(out.shape[0] // step):
        rows = pl.ds(i * step, step)
        out[rows, :] = lax.dot_general(
            held[rows, :], w[...], (((1,), (1,)), ((), ())), preferred_element_type=F32
        ).astype(BF16)


def call(kernel, outs, scratch, flops, *args):
    vmem = pl.BlockSpec(memory_space=pltpu.VMEM)
    return pl.pallas_call(
        kernel,
        out_shape=outs,
        in_specs=[pl.BlockSpec(memory_space=pltpu.SMEM)] + [vmem] * (len(args) - 1),
        out_specs=[vmem] * len(outs),
        scratch_shapes=scratch,
        compiler_params=pltpu.CompilerParams(vmem_limit_bytes=32 * 1024 * 1024),
        cost_estimate=pl.CostEstimate(
            flops=flops, bytes_accessed=6 * 1024 * 1024, transcendentals=0
        ),
    )(*args)


def total(parts):
    parts = [p.astype(F32) for p in parts]
    return functools.reduce(lambda a, b: a + b, parts)


def shards(acts, weight, cotangent):
    row, col = lax.axis_index("row"), lax.axis_index("col")
    me = jnp.stack([row, col]).astype(jnp.int32)
    high = ((row >> 1) & 1) == 1
    part, depth = acts.shape
    width = weight.shape[1]
    tokens = part * COLS

    pair = jnp.concatenate([acts, swap(acts, "col", 16)])
    line = jnp.concatenate([pair] + [swap(pair, "col", 4 * k) for k in (1, 2, 3)])
    x3 = swap(line, "col", 3)
    x2 = swap(line, "col", 2)
    x1 = swap(line, "col", 1)
    other = swap(cotangent, "row", 2)

    flops = 2 * tokens * depth * width
    send, keep, acts_full = call(
        up_kernel,
        [
            jax.ShapeDtypeStruct((tokens // 2, width), BF16),
            jax.ShapeDtypeStruct((tokens // 2, width), F32),
            jax.ShapeDtypeStruct((tokens, depth), BF16),
        ],
        [],
        flops,
        me, line, x1, x2, x3, weight, other,
    )

    mine = (keep + swap(send, "row", 1).astype(F32)).astype(BF16)
    size = tokens // 8
    got = spread(mine, "row", Y_GROUPS)
    mine = total([got[y * size : (y + 1) * size] for y in range(4)])
    pre = mine + swap(mine.astype(BF16), "row", 2).astype(F32)

    size = tokens // 16
    both = jnp.concatenate(
        [jnp.where(high, other, cotangent), jnp.where(high, cotangent, other)]
    )
    output = gelu_value(jnp.where(high, pre[size:], pre[:size])).astype(BF16)
    grad = (both.astype(F32) * gelu_slope(pre)).astype(BF16)

    g0 = lax.all_gather(grad, "row", axis=0, tiled=True, axis_index_groups=Y_GROUPS)
    g1 = swap(g0, "row", 1)

    (partial,) = call(
        down_kernel,
        [jax.ShapeDtypeStruct((tokens, depth), BF16)],
        [pltpu.VMEM((tokens, width), BF16)],
        flops,
        me, g0, g1, weight,
    )

    size = tokens // 4
    got = spread(partial, "col", X_GROUPS)
    mine = total([got[x * size : (x + 1) * size] for x in range(4)])
    size = tokens // 16
    sent = [mine[k * size : (k + 1) * size].astype(BF16) for k in (1, 2, 3)]
    got = [swap(s, "col", 4 * k) for s, k in zip(sent, (1, 2, 3))]
    mine = total([mine[:size]] + got)
    size = tokens // 32
    acts_grad = total([mine[:size], swap(mine[size:].astype(BF16), "col", 16)]).astype(BF16)

    grad_full = jnp.concatenate([g0, g1])
    weight_sum = lax.dot_general(
        acts_full, grad_full, (((0,), (0,)), ((), ())), preferred_element_type=F32
    )
    weight_grad = (weight_sum * tokens ** (-0.5)).astype(BF16)
    return (output, acts_grad, weight_grad)


def solution(mesh):
    in_specs = (P("col", "row"), P("row", "col"), P("row", "col"))
    out_specs = (P("row", "col"), P("col", "row"), P("row", "col"))
    return jax.shard_map(shards, mesh=mesh, in_specs=in_specs, out_specs=out_specs, check_vma=False)
```

```python
import functools
import math

import jax
import jax.numpy as jnp
from jax import lax
from jax.experimental import pallas as pl
from jax.experimental.pallas import tpu as pltpu
from jax.sharding import PartitionSpec as P

ROWS, COLS = 16, 32
F32, BF16 = jnp.float32, jnp.bfloat16
Y_GROUPS = [[y * 4 + low for y in range(4)] for low in range(4)]
Z_GROUPS = [[(h * 4 + z) * 4 + x for z in range(4)] for h in range(2) for x in range(4)]


def gelu_value(pre):
    return 0.5 * pre * (1.0 + lax.erf(pre / math.sqrt(2.0)))


def gelu_slope(pre):
    return 0.5 * (1.0 + lax.erf(pre / math.sqrt(2.0))) + pre * jnp.exp(
        -0.5 * pre * pre
    ) / math.sqrt(2.0 * math.pi)


def swap(value, axis, mask):
    size = ROWS if axis == "row" else COLS
    return lax.ppermute(value, axis, [(i, i ^ mask) for i in range(size)])


def spread(value, axis, groups):
    return lax.all_to_all(
        value, axis, split_axis=0, concat_axis=0, axis_index_groups=groups, tiled=True
    )


def total(parts):
    parts = [p.astype(F32) for p in parts]
    return functools.reduce(lambda a, b: a + b, parts)


def line_place(z, me_col):
    return (z & 3) * 2 + ((z >> 2) ^ (me_col >> 4))


def own_first(me):
    return ((me[0] ^ (me[1] >> 1)) & 1) == 0


def products(me, piece, weights, held, out):
    part = held.shape[0] // 8
    for z in range(8):
        src = pl.multiple_of(line_place(z, me[1]) * part, part)
        held[pl.ds(z * part, part), :] = piece[pl.ds(src, part), :]
    for block, w in enumerate(weights):
        value = jnp.dot(held[...], w[...], preferred_element_type=F32)
        for z in range(8):
            out[pl.ds((z * 2 + block) * part, part), :] = value[z * part : (z + 1) * part]


def early_kernel(me, piece, w0, w1, out, held):
    products(me, piece, (w0, w1), held, out)


def send_kernel(me, early, piece, _, w0, w1, late, send, held):
    products(me, piece, (w0, w1), held, late)

    @pl.when(own_first(me))
    def _():
        send[...] = late[...].astype(BF16)

    @pl.when(jnp.logical_not(own_first(me)))
    def _():
        send[...] = early[...].astype(BF16)


def keep_kernel(me, early, late, got, out):
    @pl.when(own_first(me))
    def _():
        out[...] = (early[...] + got[...].astype(F32)).astype(BF16)

    @pl.when(jnp.logical_not(own_first(me)))
    def _():
        out[...] = (late[...] + got[...].astype(F32)).astype(BF16)


def order_kernel(me, line, across, out):
    half = line.shape[0]
    part = half // 8
    swapped = (me[0] ^ (me[1] >> 1)) & 1
    for s, piece in enumerate((line, across)):
        for z in range(8):
            src = pl.multiple_of(line_place(z, me[1]) * part, part)
            to = pl.multiple_of((s ^ swapped) * half + z * part, part)
            out[pl.ds(to, part), :] = piece[pl.ds(src, part), :]


def back(me, grad, weights, held):
    size = held.shape[1]
    part = size // 8
    for z in range(8):
        to = pl.multiple_of(line_place(z, me[1]) * part, part)
        for block in range(2):
            held[block, pl.ds(to, part), :] = grad[pl.ds((z * 2 + block) * part, part), :]
    values = [
        lax.dot_general(
            held[block], w[...], (((1,), (1,)), ((), ())), preferred_element_type=F32
        )
        for block, w in enumerate(weights)
    ]
    return values[0] + values[1]


def first_kernel(me, grad, _, w0, w1, out, held):
    out[...] = back(me, grad, (w0, w1), held)


def second_kernel(me, first, grad, w0, w1, keep, send, held):
    value = back(me, grad, (w0, w1), held)

    @pl.when(own_first(me))
    def _():
        keep[...] = first[...]
        send[...] = value.astype(BF16)

    @pl.when(jnp.logical_not(own_first(me)))
    def _():
        keep[...] = value
        send[...] = first[...].astype(BF16)


def call(kernel, outs, scratch, flops, *args):
    vmem = pl.BlockSpec(memory_space=pltpu.VMEM)
    return pl.pallas_call(
        kernel,
        out_shape=outs,
        in_specs=[pl.BlockSpec(memory_space=pltpu.SMEM)] + [vmem] * (len(args) - 1),
        out_specs=[vmem] * len(outs),
        scratch_shapes=scratch,
        compiler_params=pltpu.CompilerParams(vmem_limit_bytes=32 * 1024 * 1024),
        cost_estimate=pl.CostEstimate(
            flops=flops, bytes_accessed=3 * 1024 * 1024, transcendentals=0
        ),
    )(*args)


def shape(rows, columns, dtype):
    return jax.ShapeDtypeStruct((rows, columns), dtype)


def shards(acts, weight, cotangent):
    row, col = lax.axis_index("row"), lax.axis_index("col")
    me = jnp.stack([row, col]).astype(jnp.int32)
    upper = ((row >> 1) & 1) == 1
    odd = (col & 1) == 1
    part, depth = acts.shape
    width = weight.shape[1]
    tokens = part * COLS
    flops = tokens * depth * width

    pair = jnp.concatenate([acts, swap(acts, "col", 16)])
    partner = swap(weight, "col", 1)
    line = lax.all_gather(pair, "col", axis=0, tiled=True, axis_index_groups=Z_GROUPS)
    across = swap(line, "col", 2)

    other = swap(cotangent, "row", 2)
    low = jnp.stack([jnp.where(upper, x, y) for x, y in ((other, cotangent), (cotangent, other))])
    low, high = low[:, :part], low[:, part:]
    both = [jnp.where(odd, high, low), swap(jnp.where(odd, low, high), "col", 1)]
    both = jnp.stack(both, axis=1).reshape(4 * part, width)

    size = tokens // 2
    held = [pltpu.VMEM((tokens // 4, depth), BF16)]
    (early,) = call(
        early_kernel, [shape(size, width, F32)], held, flops, me, line, weight, partner
    )
    late, send = call(
        send_kernel,
        [shape(size, width, F32), shape(size, width, BF16)],
        held, flops, me, early, across, other, weight, partner,
    )

    (mine,) = call(
        keep_kernel,
        [shape(size, width, BF16)],
        [], size * width, me, early, late, swap(send, "row", 1),
    )
    size = tokens // 8
    got = spread(mine, "row", Y_GROUPS)
    mine = total([got[y * size : (y + 1) * size] for y in range(4)])
    pre = mine + swap(mine.astype(BF16), "row", 2).astype(F32)

    size = tokens // 16
    value = gelu_value(jnp.where(upper, pre[size:], pre[:size])).astype(BF16)
    grad = (both.astype(F32) * gelu_slope(pre)).astype(BF16)
    mine, got = value[:part], swap(value[part:], "col", 1)
    output = jnp.concatenate([jnp.where(odd, got, mine), jnp.where(odd, mine, got)])

    g0 = lax.all_gather(grad, "row", axis=0, tiled=True, axis_index_groups=Y_GROUPS)
    g1 = swap(g0, "row", 1)

    size = tokens // 2
    (near,) = call(order_kernel, [shape(size, depth, BF16)], [], 0, me, line, across)
    far = swap(near, "col", 1)

    size = tokens // 4
    held = [pltpu.VMEM((2, size, width), BF16)]
    (first,) = call(
        first_kernel,
        [shape(size, depth, F32)],
        held, flops, me, g0, far, weight, partner,
    )
    keep, send = call(
        second_kernel,
        [shape(size, depth, F32), shape(size, depth, BF16)],
        held, flops, me, first, g1, weight, partner,
    )

    mine = total([keep, swap(send, "col", 2)]).astype(BF16)
    size = tokens // 16
    got = spread(mine, "col", Z_GROUPS)
    mine = total([got[k * size : (k + 1) * size] for k in range(4)])
    acts_grad = total([mine[:part], swap(mine[part:].astype(BF16), "col", 16)]).astype(BF16)

    split = [g.reshape(8, 2, part, width) for g in (g0, g1)]
    own = [s[:, 0].reshape(-1, width) for s in split]
    others = jnp.concatenate([s[:, 1].reshape(-1, width) for s in split])
    weight_sum = lax.dot_general(
        jnp.concatenate([near, far]),
        jnp.concatenate(own + [swap(others, "col", 1)]),
        (((0,), (0,)), ((), ())),
        preferred_element_type=F32,
    )
    weight_grad = (weight_sum * tokens ** (-0.5)).astype(BF16)
    return (output, acts_grad, weight_grad)


def solution(mesh):
    in_specs = (P("col", "row"), P("row", "col"), P("row", "col"))
    out_specs = (P("row", "col"), P("col", "row"), P("row", "col"))
    return jax.shard_map(shards, mesh=mesh, in_specs=in_specs, out_specs=out_specs, check_vma=False)
```

```python
import functools
import math

import jax
import jax.numpy as jnp
from jax import lax
from jax.experimental import pallas as pl
from jax.experimental.pallas import tpu as pltpu
from jax.sharding import PartitionSpec as P

ROWS, COLS = 16, 32
F32, BF16 = jnp.float32, jnp.bfloat16
Y_GROUPS = [[y * 4 + low for y in range(4)] for low in range(4)]
Z_GROUPS = [[(h * 4 + z) * 4 + x for z in range(4)] for h in range(2) for x in range(4)]


def gelu_value(pre):
    return 0.5 * pre * (1.0 + lax.erf(pre / math.sqrt(2.0)))


def gelu_slope(pre):
    return 0.5 * (1.0 + lax.erf(pre / math.sqrt(2.0))) + pre * jnp.exp(
        -0.5 * pre * pre
    ) / math.sqrt(2.0 * math.pi)


def swap(value, axis, mask):
    size = ROWS if axis == "row" else COLS
    return lax.ppermute(value, axis, [(i, i ^ mask) for i in range(size)])


def spread(value, axis, groups):
    return lax.all_to_all(
        value, axis, split_axis=0, concat_axis=0, axis_index_groups=groups, tiled=True
    )


def total(parts):
    parts = [p.astype(F32) for p in parts]
    return functools.reduce(lambda a, b: a + b, parts)


def line_place(z, me_col):
    return (z & 3) * 2 + ((z >> 2) ^ (me_col >> 4))


def own_first(me):
    return ((me[0] ^ (me[1] >> 1)) & 1) == 0


def products(me, piece, weights, held, out):
    part = held.shape[0] // 8
    for z in range(8):
        src = pl.multiple_of(line_place(z, me[1]) * part, part)
        held[pl.ds(z * part, part), :] = piece[pl.ds(src, part), :]
    for block, w in enumerate(weights):
        value = jnp.dot(held[...], w[...], preferred_element_type=F32)
        for z in range(8):
            out[pl.ds((z * 2 + block) * part, part), :] = value[z * part : (z + 1) * part]


def early_kernel(me, piece, w0, w1, cotangent, out, passed, held):
    passed[...] = cotangent[...]
    products(me, piece, (w0, w1), held, out)


def send_kernel(me, early, piece, _, w0, w1, late, send, held):
    products(me, piece, (w0, w1), held, late)

    @pl.when(own_first(me))
    def _():
        send[...] = late[...].astype(BF16)

    @pl.when(jnp.logical_not(own_first(me)))
    def _():
        send[...] = early[...].astype(BF16)


def keep_kernel(me, early, late, got, out):
    @pl.when(own_first(me))
    def _():
        out[...] = (early[...] + got[...].astype(F32)).astype(BF16)

    @pl.when(jnp.logical_not(own_first(me)))
    def _():
        out[...] = (late[...] + got[...].astype(F32)).astype(BF16)


def order_kernel(me, line, across, out):
    half = line.shape[0]
    part = half // 8
    swapped = (me[0] ^ (me[1] >> 1)) & 1
    for s, piece in enumerate((line, across)):
        for z in range(8):
            src = pl.multiple_of(line_place(z, me[1]) * part, part)
            to = pl.multiple_of((s ^ swapped) * half + z * part, part)
            out[pl.ds(to, part), :] = piece[pl.ds(src, part), :]


def back(me, grad, weights, held):
    size = held.shape[1]
    part = size // 8
    for z in range(8):
        to = pl.multiple_of(line_place(z, me[1]) * part, part)
        for block in range(2):
            held[block, pl.ds(to, part), :] = grad[pl.ds((z * 2 + block) * part, part), :]
    values = [
        lax.dot_general(
            held[block], w[...], (((1,), (1,)), ((), ())), preferred_element_type=F32
        )
        for block, w in enumerate(weights)
    ]
    return values[0] + values[1]


def first_kernel(me, grad, _, w0, w1, out, held):
    out[...] = back(me, grad, (w0, w1), held)


def second_kernel(me, first, grad, w0, w1, keep, send, held):
    value = back(me, grad, (w0, w1), held)

    @pl.when(own_first(me))
    def _():
        keep[...] = first[...]
        send[...] = value.astype(BF16)

    @pl.when(jnp.logical_not(own_first(me)))
    def _():
        keep[...] = value
        send[...] = first[...].astype(BF16)


def call(kernel, outs, scratch, flops, *args):
    vmem = pl.BlockSpec(memory_space=pltpu.VMEM)
    return pl.pallas_call(
        kernel,
        out_shape=outs,
        in_specs=[pl.BlockSpec(memory_space=pltpu.SMEM)] + [vmem] * (len(args) - 1),
        out_specs=[vmem] * len(outs),
        scratch_shapes=scratch,
        compiler_params=pltpu.CompilerParams(vmem_limit_bytes=32 * 1024 * 1024),
        cost_estimate=pl.CostEstimate(
            flops=flops, bytes_accessed=3 * 1024 * 1024, transcendentals=0
        ),
    )(*args)


def shape(rows, columns, dtype):
    return jax.ShapeDtypeStruct((rows, columns), dtype)


def shards(acts, weight, cotangent):
    row, col = lax.axis_index("row"), lax.axis_index("col")
    me = jnp.stack([row, col]).astype(jnp.int32)
    upper = ((row >> 1) & 1) == 1
    odd = (col & 1) == 1
    part, depth = acts.shape
    width = weight.shape[1]
    tokens = part * COLS
    flops = tokens * depth * width

    pair = jnp.concatenate([acts, swap(acts, "col", 16)])
    partner = swap(weight, "col", 1)
    line = lax.all_gather(pair, "col", axis=0, tiled=True, axis_index_groups=Z_GROUPS)
    across = swap(line, "col", 2)

    size = tokens // 2
    held = [pltpu.VMEM((tokens // 4, depth), BF16)]
    early, passed = call(
        early_kernel,
        [shape(size, width, F32), shape(2 * part, width, BF16)],
        held, flops, me, line, weight, partner, cotangent,
    )

    other = swap(passed, "row", 2)
    pairs = [jnp.where(upper, a, b) for a, b in ((other, cotangent), (cotangent, other))]
    mine = [jnp.where(odd, p[part:], p[:part]) for p in pairs]
    got = swap(jnp.concatenate([jnp.where(odd, p[:part], p[part:]) for p in pairs]), "col", 1)
    both = jnp.concatenate([mine[0], got[:part], mine[1], got[part:]])

    late, send = call(
        send_kernel,
        [shape(size, width, F32), shape(size, width, BF16)],
        held, flops, me, early, across, other, weight, partner,
    )

    (mine,) = call(
        keep_kernel,
        [shape(size, width, BF16)],
        [], size * width, me, early, late, swap(send, "row", 1),
    )
    size = tokens // 8
    got = spread(mine, "row", Y_GROUPS)
    mine = total([got[y * size : (y + 1) * size] for y in range(4)])
    pre = mine + swap(mine.astype(BF16), "row", 2).astype(F32)

    size = tokens // 16
    value = gelu_value(jnp.where(upper, pre[size:], pre[:size])).astype(BF16)
    grad = (both.astype(F32) * gelu_slope(pre)).astype(BF16)
    mine, got = value[:part], swap(value[part:], "col", 1)
    output = jnp.concatenate([jnp.where(odd, got, mine), jnp.where(odd, mine, got)])

    g0 = lax.all_gather(grad, "row", axis=0, tiled=True, axis_index_groups=Y_GROUPS)
    g1 = swap(g0, "row", 1)

    size = tokens // 2
    (near,) = call(order_kernel, [shape(size, depth, BF16)], [], 0, me, line, across)
    far = swap(near, "col", 1)

    size = tokens // 4
    held = [pltpu.VMEM((2, size, width), BF16)]
    (first,) = call(
        first_kernel,
        [shape(size, depth, F32)],
        held, flops, me, g0, far, weight, partner,
    )
    keep, send = call(
        second_kernel,
        [shape(size, depth, F32), shape(size, depth, BF16)],
        held, flops, me, first, g1, weight, partner,
    )

    mine = total([keep, swap(send, "col", 2)]).astype(BF16)
    size = tokens // 16
    got = spread(mine, "col", Z_GROUPS)
    mine = total([got[k * size : (k + 1) * size] for k in range(4)])
    acts_grad = total([mine[:part], swap(mine[part:].astype(BF16), "col", 16)]).astype(BF16)

    split = [g.reshape(8, 2, part, width) for g in (g0, g1)]
    own = [g[:, 0].reshape(-1, width) for g in split]
    others = [swap(split[0][:, 1].reshape(-1, width), "col", 1)]
    others += [swap(others[0], "row", 1)]
    weight_sum = lax.dot_general(
        jnp.concatenate([near, far]),
        jnp.concatenate(own + others),
        (((0,), (0,)), ((), ())),
        preferred_element_type=F32,
    )
    weight_grad = (weight_sum * tokens ** (-0.5)).astype(BF16)
    return (output, acts_grad, weight_grad)


def solution(mesh):
    in_specs = (P("col", "row"), P("row", "col"), P("row", "col"))
    out_specs = (P("row", "col"), P("col", "row"), P("row", "col"))
    return jax.shard_map(shards, mesh=mesh, in_specs=in_specs, out_specs=out_specs, check_vma=False)
```

```python
import functools
import math

import jax
import jax.numpy as jnp
from jax import lax
from jax.experimental import pallas as pl
from jax.experimental.pallas import tpu as pltpu
from jax.sharding import PartitionSpec as P

ROWS, COLS = 16, 32
F32, BF16 = jnp.float32, jnp.bfloat16
Y_GROUPS = [[y * 4 + low for y in range(4)] for low in range(4)]
Z_GROUPS = [[(h * 4 + z) * 4 + x for z in range(4)] for h in range(2) for x in range(4)]


def gelu_value(pre):
    return 0.5 * pre * (1.0 + lax.erf(pre / math.sqrt(2.0)))


def gelu_slope(pre):
    return 0.5 * (1.0 + lax.erf(pre / math.sqrt(2.0))) + pre * jnp.exp(
        -0.5 * pre * pre
    ) / math.sqrt(2.0 * math.pi)


def swap(value, axis, mask):
    size = ROWS if axis == "row" else COLS
    return lax.ppermute(value, axis, [(i, i ^ mask) for i in range(size)])


def spread(value, axis, groups):
    return lax.all_to_all(
        value, axis, split_axis=0, concat_axis=0, axis_index_groups=groups, tiled=True
    )


def total(parts):
    parts = [p.astype(F32) for p in parts]
    return functools.reduce(lambda a, b: a + b, parts)


def line_place(z, me_col):
    return (z & 3) * 2 + ((z >> 2) ^ (me_col >> 4))


def own_first(me):
    return ((me[0] ^ (me[1] >> 1)) & 1) == 0


def products(me, piece, weights, held, out):
    part = held.shape[0] // 8
    for z in range(8):
        src = pl.multiple_of(line_place(z, me[1]) * part, part)
        held[pl.ds(z * part, part), :] = piece[pl.ds(src, part), :]
    for block, w in enumerate(weights):
        value = jnp.dot(held[...], w[...], preferred_element_type=F32)
        for z in range(8):
            out[pl.ds((z * 2 + block) * part, part), :] = value[z * part : (z + 1) * part]


def early_kernel(me, piece, w0, w1, out, held):
    products(me, piece, (w0, w1), held, out)


def send_kernel(me, early, piece, _, w0, w1, late, send, held):
    products(me, piece, (w0, w1), held, late)

    @pl.when(own_first(me))
    def _():
        send[...] = late[...].astype(BF16)

    @pl.when(jnp.logical_not(own_first(me)))
    def _():
        send[...] = early[...].astype(BF16)


def keep_kernel(me, early, late, got, out):
    @pl.when(own_first(me))
    def _():
        out[...] = (early[...] + got[...].astype(F32)).astype(BF16)

    @pl.when(jnp.logical_not(own_first(me)))
    def _():
        out[...] = (late[...] + got[...].astype(F32)).astype(BF16)


def stack_kernel(me, mine0, mine1, got, out):
    part = mine0.shape[0]
    out[:part] = mine0[...]
    out[part : 2 * part] = got[:part]
    out[2 * part : 3 * part] = mine1[...]
    out[3 * part :] = got[part:]


def sum_kernel(me, mine, got, _, out):
    out[...] = (mine[...] + got[...].astype(F32)).astype(BF16)


def order_kernel(me, line, across, _, out):
    half = line.shape[0]
    part = half // 8
    swapped = (me[0] ^ (me[1] >> 1)) & 1
    for s, piece in enumerate((line, across)):
        for z in range(8):
            src = pl.multiple_of(line_place(z, me[1]) * part, part)
            to = pl.multiple_of((s ^ swapped) * half + z * part, part)
            out[pl.ds(to, part), :] = piece[pl.ds(src, part), :]


def back(me, grad, weights, held):
    size = held.shape[1]
    part = size // 8
    for z in range(8):
        to = pl.multiple_of(line_place(z, me[1]) * part, part)
        for block in range(2):
            held[block, pl.ds(to, part), :] = grad[pl.ds((z * 2 + block) * part, part), :]
    values = [
        lax.dot_general(
            held[block], w[...], (((1,), (1,)), ((), ())), preferred_element_type=F32
        )
        for block, w in enumerate(weights)
    ]
    return values[0] + values[1]


def first_kernel(me, grad, _, w0, w1, out, held):
    out[...] = back(me, grad, (w0, w1), held)


def second_kernel(me, first, grad, w0, w1, keep, send, held):
    value = back(me, grad, (w0, w1), held)

    @pl.when(own_first(me))
    def _():
        keep[...] = first[...]
        send[...] = value.astype(BF16)

    @pl.when(jnp.logical_not(own_first(me)))
    def _():
        keep[...] = value
        send[...] = first[...].astype(BF16)


def call(kernel, outs, scratch, flops, *args):
    vmem = pl.BlockSpec(memory_space=pltpu.VMEM)
    return pl.pallas_call(
        kernel,
        out_shape=outs,
        in_specs=[pl.BlockSpec(memory_space=pltpu.SMEM)] + [vmem] * (len(args) - 1),
        out_specs=[vmem] * len(outs),
        scratch_shapes=scratch,
        compiler_params=pltpu.CompilerParams(vmem_limit_bytes=12 * 1024 * 1024),
        cost_estimate=pl.CostEstimate(
            flops=flops, bytes_accessed=3 * 1024 * 1024, transcendentals=0
        ),
    )(*args)


def shape(rows, columns, dtype):
    return jax.ShapeDtypeStruct((rows, columns), dtype)


def shards(acts, weight, cotangent):
    row, col = lax.axis_index("row"), lax.axis_index("col")
    me = jnp.stack([row, col]).astype(jnp.int32)
    upper = ((row >> 1) & 1) == 1
    odd = (col & 1) == 1
    part, depth = acts.shape
    width = weight.shape[1]
    tokens = part * COLS
    flops = tokens * depth * width

    pair = jnp.concatenate([acts, swap(acts, "col", 16)])
    partner = swap(weight, "col", 1)
    line = lax.all_gather(pair, "col", axis=0, tiled=True, axis_index_groups=Z_GROUPS)
    across = swap(line, "col", 2)

    size = tokens // 2
    held = [pltpu.VMEM((tokens // 4, depth), BF16)]
    (early,) = call(
        early_kernel, [shape(size, width, F32)], held, flops, me, line, weight, partner
    )

    other = swap(cotangent, "row", 2)
    pairs = [jnp.where(upper, a, b) for a, b in ((other, cotangent), (cotangent, other))]
    mine = [jnp.where(odd, p[part:], p[:part]) for p in pairs]
    got = swap(jnp.concatenate([jnp.where(odd, p[:part], p[part:]) for p in pairs]), "col", 1)
    (both,) = call(stack_kernel, [shape(4 * part, width, BF16)], [], 0, me, *mine, got)

    late, send = call(
        send_kernel,
        [shape(size, width, F32), shape(size, width, BF16)],
        held, flops, me, early, across, other, weight, partner,
    )

    (mine,) = call(
        keep_kernel,
        [shape(size, width, BF16)],
        [], size * width, me, early, late, swap(send, "row", 1),
    )
    size = tokens // 8
    got = spread(mine, "row", Y_GROUPS)
    mine = total([got[y * size : (y + 1) * size] for y in range(4)])
    sent = mine.astype(BF16)
    pre = mine + swap(sent, "row", 2).astype(F32)

    size = tokens // 16
    value = gelu_value(jnp.where(upper, pre[size:], pre[:size])).astype(BF16)
    grad = (both.astype(F32) * gelu_slope(pre)).astype(BF16)
    mine, fetched = value[:part], swap(value[part:], "col", 1)
    output = jnp.concatenate([jnp.where(odd, fetched, mine), jnp.where(odd, mine, fetched)])

    g0 = lax.all_gather(grad, "row", axis=0, tiled=True, axis_index_groups=Y_GROUPS)
    g1 = swap(g0, "row", 1)

    size = tokens // 2
    (near,) = call(order_kernel, [shape(size, depth, BF16)], [], 0, me, line, across, sent)
    far = swap(near, "col", 1)

    size = tokens // 4
    held = [pltpu.VMEM((2, size, width), BF16)]
    (first,) = call(
        first_kernel,
        [shape(size, depth, F32)],
        held, flops, me, g0, far, weight, partner,
    )
    keep, send = call(
        second_kernel,
        [shape(size, depth, F32), shape(size, depth, BF16)],
        held, flops, me, first, g1, weight, partner,
    )

    (mine,) = call(
        sum_kernel, [shape(size, depth, BF16)], [], size * depth,
        me, keep, swap(send, "col", 2), fetched,
    )
    size = tokens // 16
    got = spread(mine, "col", Z_GROUPS)
    mine = total([got[k * size : (k + 1) * size] for k in range(4)])
    acts_grad = total([mine[:part], swap(mine[part:].astype(BF16), "col", 16)]).astype(BF16)

    split = [g.reshape(8, 2, part, width) for g in (g0, g1)]
    own = [g[:, 0].reshape(-1, width) for g in split]
    others = [swap(split[0][:, 1].reshape(-1, width), "col", 1)]
    others += [swap(others[0], "row", 1)]
    weight_sum = lax.dot_general(
        jnp.concatenate([near, far]),
        jnp.concatenate(own + others),
        (((0,), (0,)), ((), ())),
        preferred_element_type=F32,
    )
    weight_grad = (weight_sum * tokens ** (-0.5)).astype(BF16)
    return (output, acts_grad, weight_grad)


def solution(mesh):
    in_specs = (P("col", "row"), P("row", "col"), P("row", "col"))
    out_specs = (P("row", "col"), P("col", "row"), P("row", "col"))
    return jax.shard_map(shards, mesh=mesh, in_specs=in_specs, out_specs=out_specs, check_vma=False)
```

```python
import functools
import math

import jax
import jax.numpy as jnp
from jax import lax
from jax.experimental import pallas as pl
from jax.experimental.pallas import tpu as pltpu
from jax.sharding import PartitionSpec as P

ROWS, COLS = 16, 32
F32, BF16 = jnp.float32, jnp.bfloat16
Y_GROUPS = [[y * 4 + low for y in range(4)] for low in range(4)]
Z_GROUPS = [[(h * 4 + z) * 4 + x for z in range(4)] for h in range(2) for x in range(4)]


def gelu_value(pre):
    return 0.5 * pre * (1.0 + lax.erf(pre / math.sqrt(2.0)))


def gelu_slope(pre):
    return 0.5 * (1.0 + lax.erf(pre / math.sqrt(2.0))) + pre * jnp.exp(
        -0.5 * pre * pre
    ) / math.sqrt(2.0 * math.pi)


def swap(value, axis, mask):
    size = ROWS if axis == "row" else COLS
    return lax.ppermute(value, axis, [(i, i ^ mask) for i in range(size)])


def spread(value, axis, groups):
    return lax.all_to_all(
        value, axis, split_axis=0, concat_axis=0, axis_index_groups=groups, tiled=True
    )


def total(parts):
    parts = [p.astype(F32) for p in parts]
    return functools.reduce(lambda a, b: a + b, parts)


def line_place(z, me_col):
    return (z & 3) * 2 + ((z >> 2) ^ (me_col >> 4))


def own_first(me):
    return ((me[0] ^ (me[1] >> 1)) & 1) == 0


def products(me, piece, weights, held, out):
    part = held.shape[0] // 8
    for z in range(8):
        src = pl.multiple_of(line_place(z, me[1]) * part, part)
        held[pl.ds(z * part, part), :] = piece[pl.ds(src, part), :]
    for block, w in enumerate(weights):
        value = jnp.dot(held[...], w[...], preferred_element_type=F32)
        for z in range(8):
            out[pl.ds((z * 2 + block) * part, part), :] = value[z * part : (z + 1) * part]


def early_kernel(me, piece, w0, w1, out, held):
    products(me, piece, (w0, w1), held, out)


def send_kernel(me, early, piece, _, w0, w1, late, send, held):
    products(me, piece, (w0, w1), held, late)

    @pl.when(own_first(me))
    def _():
        send[...] = late[...].astype(BF16)

    @pl.when(jnp.logical_not(own_first(me)))
    def _():
        send[...] = early[...].astype(BF16)


def keep_kernel(me, early, late, got, out):
    @pl.when(own_first(me))
    def _():
        out[...] = (early[...] + got[...].astype(F32)).astype(BF16)

    @pl.when(jnp.logical_not(own_first(me)))
    def _():
        out[...] = (late[...] + got[...].astype(F32)).astype(BF16)


def stack_kernel(me, mine0, mine1, got, value, out, passed):
    passed[...] = value[...]
    part = mine0.shape[0]
    out[:part] = mine0[...]
    out[part : 2 * part] = got[:part]
    out[2 * part : 3 * part] = mine1[...]
    out[3 * part :] = got[part:]


def order_kernel(me, line, across, _, out):
    half = line.shape[0]
    part = half // 8
    swapped = (me[0] ^ (me[1] >> 1)) & 1
    for s, piece in enumerate((line, across)):
        for z in range(8):
            src = pl.multiple_of(line_place(z, me[1]) * part, part)
            to = pl.multiple_of((s ^ swapped) * half + z * part, part)
            out[pl.ds(to, part), :] = piece[pl.ds(src, part), :]


def back(me, grad, weights, held):
    size = held.shape[1]
    part = size // 8
    for z in range(8):
        to = pl.multiple_of(line_place(z, me[1]) * part, part)
        for block in range(2):
            held[block, pl.ds(to, part), :] = grad[pl.ds((z * 2 + block) * part, part), :]
    values = [
        lax.dot_general(
            held[block], w[...], (((1,), (1,)), ((), ())), preferred_element_type=F32
        )
        for block, w in enumerate(weights)
    ]
    return values[0] + values[1]


def first_kernel(me, grad, _, w0, w1, out, held):
    out[...] = back(me, grad, (w0, w1), held)


def second_kernel(me, first, grad, w0, w1, keep, send, held):
    value = back(me, grad, (w0, w1), held)

    @pl.when(own_first(me))
    def _():
        keep[...] = first[...]
        send[...] = value.astype(BF16)

    @pl.when(jnp.logical_not(own_first(me)))
    def _():
        keep[...] = value
        send[...] = first[...].astype(BF16)


def call(kernel, outs, scratch, flops, *args):
    vmem = pl.BlockSpec(memory_space=pltpu.VMEM)
    return pl.pallas_call(
        kernel,
        out_shape=outs,
        in_specs=[pl.BlockSpec(memory_space=pltpu.SMEM)] + [vmem] * (len(args) - 1),
        out_specs=[vmem] * len(outs),
        scratch_shapes=scratch,
        compiler_params=pltpu.CompilerParams(vmem_limit_bytes=12 * 1024 * 1024),
        cost_estimate=pl.CostEstimate(
            flops=flops, bytes_accessed=3 * 1024 * 1024, transcendentals=0
        ),
    )(*args)


def shape(rows, columns, dtype):
    return jax.ShapeDtypeStruct((rows, columns), dtype)


def shards(acts, weight, cotangent):
    row, col = lax.axis_index("row"), lax.axis_index("col")
    me = jnp.stack([row, col]).astype(jnp.int32)
    upper = ((row >> 1) & 1) == 1
    odd = (col & 1) == 1
    part, depth = acts.shape
    width = weight.shape[1]
    tokens = part * COLS
    flops = tokens * depth * width

    pair = jnp.concatenate([acts, swap(acts, "col", 16)])
    partner = swap(weight, "col", 1)
    line = lax.all_gather(pair, "col", axis=0, tiled=True, axis_index_groups=Z_GROUPS)
    across = swap(line, "col", 2)

    size = tokens // 2
    held = [pltpu.VMEM((tokens // 4, depth), BF16)]
    (early,) = call(
        early_kernel, [shape(size, width, F32)], held, flops, me, line, weight, partner
    )

    other = swap(cotangent, "row", 2)
    pairs = [jnp.where(upper, a, b) for a, b in ((other, cotangent), (cotangent, other))]
    mine = [jnp.where(odd, p[part:], p[:part]) for p in pairs]
    got = swap(jnp.concatenate([jnp.where(odd, p[:part], p[part:]) for p in pairs]), "col", 1)
    cotangents = [*mine, got]

    late, send = call(
        send_kernel,
        [shape(size, width, F32), shape(size, width, BF16)],
        held, flops, me, early, across, other, weight, partner,
    )

    (mine,) = call(
        keep_kernel,
        [shape(size, width, BF16)],
        [], size * width, me, early, late, swap(send, "row", 1),
    )
    size = tokens // 8
    got = spread(mine, "row", Y_GROUPS)
    mine = total([got[y * size : (y + 1) * size] for y in range(4)])
    both, sent = call(
        stack_kernel, [shape(size, width, BF16)] * 2, [], 0, me, *cotangents, mine.astype(BF16)
    )
    pre = mine + swap(sent, "row", 2).astype(F32)

    size = tokens // 16
    value = gelu_value(jnp.where(upper, pre[size:], pre[:size])).astype(BF16)
    grad = (both.astype(F32) * gelu_slope(pre)).astype(BF16)
    mine, fetched = value[:part], swap(value[part:], "col", 1)
    output = jnp.concatenate([jnp.where(odd, fetched, mine), jnp.where(odd, mine, fetched)])

    g0 = lax.all_gather(grad, "row", axis=0, tiled=True, axis_index_groups=Y_GROUPS)
    g1 = swap(g0, "row", 1)

    size = tokens // 2
    (near,) = call(order_kernel, [shape(size, depth, BF16)], [], 0, me, line, across, sent)
    far = swap(near, "col", 1)

    size = tokens // 4
    held = [pltpu.VMEM((2, size, width), BF16)]
    (first,) = call(
        first_kernel,
        [shape(size, depth, F32)],
        held, flops, me, g0, far, weight, partner,
    )
    keep, send = call(
        second_kernel,
        [shape(size, depth, F32), shape(size, depth, BF16)],
        held, flops, me, first, g1, weight, partner,
    )

    mine = total([keep, swap(send, "col", 2)]).astype(BF16)
    size = tokens // 16
    got = spread(mine, "col", Z_GROUPS)
    mine = total([got[k * size : (k + 1) * size] for k in range(4)])
    acts_grad = total([mine[:part], swap(mine[part:].astype(BF16), "col", 16)]).astype(BF16)

    split = [g.reshape(8, 2, part, width) for g in (g0, g1)]
    own = [g[:, 0].reshape(-1, width) for g in split]
    others = [swap(split[0][:, 1].reshape(-1, width), "col", 1)]
    others += [swap(others[0], "row", 1)]
    weight_sum = lax.dot_general(
        jnp.concatenate([near, far]),
        jnp.concatenate(own + others),
        (((0,), (0,)), ((), ())),
        preferred_element_type=F32,
    )
    weight_grad = (weight_sum * tokens ** (-0.5)).astype(BF16)
    return (output, acts_grad, weight_grad)


def solution(mesh):
    in_specs = (P("col", "row"), P("row", "col"), P("row", "col"))
    out_specs = (P("row", "col"), P("col", "row"), P("row", "col"))
    return jax.shard_map(shards, mesh=mesh, in_specs=in_specs, out_specs=out_specs, check_vma=False)
```

```python
import functools
import math

import jax
import jax.numpy as jnp
from jax import lax
from jax.experimental import pallas as pl
from jax.experimental.pallas import tpu as pltpu
from jax.sharding import PartitionSpec as P

ROWS, COLS = 16, 32
F32, BF16 = jnp.float32, jnp.bfloat16
Y_GROUPS = [[y * 4 + low for y in range(4)] for low in range(4)]
Z_GROUPS = [[(h * 4 + z) * 4 + x for z in range(4)] for h in range(2) for x in range(4)]


def gelu_value(pre):
    return 0.5 * pre * (1.0 + lax.erf(pre / math.sqrt(2.0)))


def gelu_slope(pre):
    return 0.5 * (1.0 + lax.erf(pre / math.sqrt(2.0))) + pre * jnp.exp(
        -0.5 * pre * pre
    ) / math.sqrt(2.0 * math.pi)


def swap(value, axis, mask):
    size = ROWS if axis == "row" else COLS
    return lax.ppermute(value, axis, [(i, i ^ mask) for i in range(size)])


def spread(value, axis, groups):
    return lax.all_to_all(
        value, axis, split_axis=0, concat_axis=0, axis_index_groups=groups, tiled=True
    )


def total(parts):
    parts = [p.astype(F32) for p in parts]
    return functools.reduce(lambda a, b: a + b, parts)


def line_place(z, me_col):
    return (z & 3) * 2 + ((z >> 2) ^ (me_col >> 4))


def own_first(me):
    return ((me[0] ^ (me[1] >> 1)) & 1) == 0


def products(me, piece, weights, held, out):
    part = held.shape[0] // 8
    for z in range(8):
        src = pl.multiple_of(line_place(z, me[1]) * part, part)
        held[pl.ds(z * part, part), :] = piece[pl.ds(src, part), :]
    for block, w in enumerate(weights):
        value = jnp.dot(held[...], w[...], preferred_element_type=F32)
        for z in range(8):
            out[pl.ds((z * 2 + block) * part, part), :] = value[z * part : (z + 1) * part]


def early_kernel(me, piece, w0, w1, out, held):
    products(me, piece, (w0, w1), held, out)


def send_kernel(me, early, piece, _, w0, w1, late, send, held):
    products(me, piece, (w0, w1), held, late)

    @pl.when(own_first(me))
    def _():
        send[...] = late[...].astype(BF16)

    @pl.when(jnp.logical_not(own_first(me)))
    def _():
        send[...] = early[...].astype(BF16)


def keep_kernel(me, early, late, got, out):
    @pl.when(own_first(me))
    def _():
        out[...] = (early[...] + got[...].astype(F32)).astype(BF16)

    @pl.when(jnp.logical_not(own_first(me)))
    def _():
        out[...] = (late[...] + got[...].astype(F32)).astype(BF16)


def stack_kernel(me, mine0, mine1, got, value, out, passed):
    passed[...] = value[...]
    part = mine0.shape[0]
    out[:part] = mine0[...]
    out[part : 2 * part] = got[:part]
    out[2 * part : 3 * part] = mine1[...]
    out[3 * part :] = got[part:]


def order_kernel(me, line, across, _, out):
    half = line.shape[0]
    part = half // 8
    swapped = (me[0] ^ (me[1] >> 1)) & 1
    for s, piece in enumerate((line, across)):
        for z in range(8):
            src = pl.multiple_of(line_place(z, me[1]) * part, part)
            to = pl.multiple_of((s ^ swapped) * half + z * part, part)
            out[pl.ds(to, part), :] = piece[pl.ds(src, part), :]


def back(me, grad, weights, held):
    size = held.shape[1]
    part = size // 8
    for z in range(8):
        to = pl.multiple_of(line_place(z, me[1]) * part, part)
        for block in range(2):
            held[block, pl.ds(to, part), :] = grad[pl.ds((z * 2 + block) * part, part), :]
    values = [
        lax.dot_general(
            held[block], w[...], (((1,), (1,)), ((), ())), preferred_element_type=F32
        )
        for block, w in enumerate(weights)
    ]
    return values[0] + values[1]


def first_kernel(me, grad, _, w0, w1, out, held):
    out[...] = back(me, grad, (w0, w1), held)


def second_kernel(me, first, grad, w0, w1, keep, send, held):
    value = back(me, grad, (w0, w1), held)

    @pl.when(own_first(me))
    def _():
        keep[...] = first[...]
        send[...] = value.astype(BF16)

    @pl.when(jnp.logical_not(own_first(me)))
    def _():
        keep[...] = value
        send[...] = first[...].astype(BF16)


def call(kernel, outs, scratch, flops, *args):
    vmem = pl.BlockSpec(memory_space=pltpu.VMEM)
    return pl.pallas_call(
        kernel,
        out_shape=outs,
        in_specs=[pl.BlockSpec(memory_space=pltpu.SMEM)] + [vmem] * (len(args) - 1),
        out_specs=[vmem] * len(outs),
        scratch_shapes=scratch,
        compiler_params=pltpu.CompilerParams(vmem_limit_bytes=12 * 1024 * 1024),
        cost_estimate=pl.CostEstimate(
            flops=flops, bytes_accessed=3 * 1024 * 1024, transcendentals=0
        ),
    )(*args)


def shape(rows, columns, dtype):
    return jax.ShapeDtypeStruct((rows, columns), dtype)


def shards(acts, weight, cotangent):
    row, col = lax.axis_index("row"), lax.axis_index("col")
    me = jnp.stack([row, col]).astype(jnp.int32)
    upper = ((row >> 1) & 1) == 1
    odd = (col & 1) == 1
    part, depth = acts.shape
    width = weight.shape[1]
    tokens = part * COLS
    flops = tokens * depth * width

    pair = jnp.concatenate([acts, swap(acts, "col", 16)])
    partner = swap(weight, "col", 1)
    line = lax.all_gather(pair, "col", axis=0, tiled=True, axis_index_groups=Z_GROUPS)
    across = swap(line, "col", 2)

    size = tokens // 2
    held = [pltpu.VMEM((tokens // 4, depth), BF16)]
    (early,) = call(
        early_kernel, [shape(size, width, F32)], held, flops, me, line, weight, partner
    )

    other = swap(cotangent, "row", 2)
    pairs = [jnp.where(upper, a, b) for a, b in ((other, cotangent), (cotangent, other))]
    mine = [jnp.where(odd, p[part:], p[:part]) for p in pairs]
    got = swap(jnp.concatenate([jnp.where(odd, p[:part], p[part:]) for p in pairs]), "col", 1)
    cotangents = [*mine, got]

    late, send = call(
        send_kernel,
        [shape(size, width, F32), shape(size, width, BF16)],
        held, flops, me, early, across, other, weight, partner,
    )

    (mine,) = call(
        keep_kernel,
        [shape(size, width, BF16)],
        [], size * width, me, early, late, swap(send, "row", 1),
    )
    size = tokens // 8
    got = spread(mine, "row", Y_GROUPS)
    mine = total([got[y * size : (y + 1) * size] for y in range(4)])
    both, sent = call(
        stack_kernel, [shape(size, width, BF16)] * 2, [], 0, me, *cotangents, mine.astype(BF16)
    )
    pre = sent.astype(F32) + swap(sent, "row", 2).astype(F32)

    size = tokens // 16
    value = gelu_value(jnp.where(upper, pre[size:], pre[:size])).astype(BF16)
    grad = (both.astype(F32) * gelu_slope(pre)).astype(BF16)
    mine, fetched = value[:part], swap(value[part:], "col", 1)
    output = jnp.concatenate([jnp.where(odd, fetched, mine), jnp.where(odd, mine, fetched)])

    g0 = lax.all_gather(grad, "row", axis=0, tiled=True, axis_index_groups=Y_GROUPS)
    g1 = swap(g0, "row", 1)

    size = tokens // 2
    (near,) = call(order_kernel, [shape(size, depth, BF16)], [], 0, me, line, across, sent)
    far = swap(near, "col", 1)

    size = tokens // 4
    held = [pltpu.VMEM((2, size, width), BF16)]
    (first,) = call(
        first_kernel,
        [shape(size, depth, F32)],
        held, flops, me, g0, far, weight, partner,
    )
    keep, send = call(
        second_kernel,
        [shape(size, depth, F32), shape(size, depth, BF16)],
        held, flops, me, first, g1, weight, partner,
    )

    mine = total([keep, swap(send, "col", 2)]).astype(BF16)
    size = tokens // 16
    got = spread(mine, "col", Z_GROUPS)
    mine = total([got[k * size : (k + 1) * size] for k in range(4)])
    acts_grad = total([mine[:part], swap(mine[part:].astype(BF16), "col", 16)]).astype(BF16)

    split = [g.reshape(8, 2, part, width) for g in (g0, g1)]
    own = [g[:, 0].reshape(-1, width) for g in split]
    others = [swap(split[0][:, 1].reshape(-1, width), "col", 1)]
    others += [swap(others[0], "row", 1)]
    weight_sum = lax.dot_general(
        jnp.concatenate([near, far]),
        jnp.concatenate(own + others),
        (((0,), (0,)), ((), ())),
        preferred_element_type=F32,
    )
    weight_grad = (weight_sum * tokens ** (-0.5)).astype(BF16)
    return (output, acts_grad, weight_grad)


def solution(mesh):
    in_specs = (P("col", "row"), P("row", "col"), P("row", "col"))
    out_specs = (P("row", "col"), P("col", "row"), P("row", "col"))
    return jax.shard_map(shards, mesh=mesh, in_specs=in_specs, out_specs=out_specs, check_vma=False)
```

```python
import functools
import math

import jax
import jax.numpy as jnp
from jax import lax
from jax.experimental import pallas as pl
from jax.experimental.pallas import tpu as pltpu
from jax.sharding import PartitionSpec as P

ROWS, COLS = 16, 32
F32, BF16 = jnp.float32, jnp.bfloat16
Y_GROUPS = [[y * 4 + low for y in range(4)] for low in range(4)]
Z_GROUPS = [[(h * 4 + z) * 4 + x for z in range(4)] for h in range(2) for x in range(4)]


def gelu_value(pre):
    return 0.5 * pre * (1.0 + lax.erf(pre / math.sqrt(2.0)))


def gelu_slope(pre):
    return 0.5 * (1.0 + lax.erf(pre / math.sqrt(2.0))) + pre * jnp.exp(
        -0.5 * pre * pre
    ) / math.sqrt(2.0 * math.pi)


def swap(value, axis, mask):
    size = ROWS if axis == "row" else COLS
    return lax.ppermute(value, axis, [(i, i ^ mask) for i in range(size)])


def spread(value, axis, groups):
    return lax.all_to_all(
        value, axis, split_axis=0, concat_axis=0, axis_index_groups=groups, tiled=True
    )


def total(parts):
    parts = [p.astype(F32) for p in parts]
    return functools.reduce(lambda a, b: a + b, parts)


def line_place(z, me_col):
    return (z & 3) * 2 + ((z >> 2) ^ (me_col >> 4))


def own_first(me):
    return ((me[0] ^ (me[1] >> 1)) & 1) == 0


def products(me, piece, weights, held, out):
    part = held.shape[0] // 8
    for z in range(8):
        src = pl.multiple_of(line_place(z, me[1]) * part, part)
        held[pl.ds(z * part, part), :] = piece[pl.ds(src, part), :]
    for block, w in enumerate(weights):
        value = jnp.dot(held[...], w[...], preferred_element_type=F32)
        for z in range(8):
            out[pl.ds((z * 2 + block) * part, part), :] = value[z * part : (z + 1) * part]


def early_kernel(me, piece, w0, w1, out, held):
    products(me, piece, (w0, w1), held, out)


def send_kernel(me, early, piece, w0, w1, late, send, held):
    products(me, piece, (w0, w1), held, late)

    @pl.when(own_first(me))
    def _():
        send[...] = late[...].astype(BF16)

    @pl.when(jnp.logical_not(own_first(me)))
    def _():
        send[...] = early[...].astype(BF16)


def keep_kernel(me, early, late, got, out):
    @pl.when(own_first(me))
    def _():
        out[...] = (early[...] + got[...].astype(F32)).astype(BF16)

    @pl.when(jnp.logical_not(own_first(me)))
    def _():
        out[...] = (late[...] + got[...].astype(F32)).astype(BF16)


def hold_kernel(me, value, out):
    out[...] = value[...]


def pick_kernel(me, own, other, _, mine, theirs):
    part = own.shape[0] // 2
    upper, odd = (me[0] >> 1) & 1, me[1] & 1
    for piece, z in ((own, upper), (other, 1 - upper)):
        to = pl.ds(pl.multiple_of(z * part, part), part)
        mine[to, :] = piece[pl.ds(pl.multiple_of(odd * part, part), part), :]
        theirs[to, :] = piece[pl.ds(pl.multiple_of((1 - odd) * part, part), part), :]


def stack_kernel(me, mine, got, out):
    part = mine.shape[0] // 2
    for z in range(2):
        out[2 * z * part : (2 * z + 1) * part] = mine[z * part : (z + 1) * part]
        out[(2 * z + 1) * part : (2 * z + 2) * part] = got[z * part : (z + 1) * part]


def order_kernel(me, line, across, _, out):
    half = line.shape[0]
    part = half // 8
    swapped = (me[0] ^ (me[1] >> 1)) & 1
    for s, piece in enumerate((line, across)):
        for z in range(8):
            src = pl.multiple_of(line_place(z, me[1]) * part, part)
            to = pl.multiple_of((s ^ swapped) * half + z * part, part)
            out[pl.ds(to, part), :] = piece[pl.ds(src, part), :]


def back(me, grad, weights, held):
    size = held.shape[1]
    part = size // 8
    for z in range(8):
        to = pl.multiple_of(line_place(z, me[1]) * part, part)
        for block in range(2):
            held[block, pl.ds(to, part), :] = grad[pl.ds((z * 2 + block) * part, part), :]
    values = [
        lax.dot_general(
            held[block], w[...], (((1,), (1,)), ((), ())), preferred_element_type=F32
        )
        for block, w in enumerate(weights)
    ]
    return values[0] + values[1]


def first_kernel(me, grad, _, w0, w1, out, held):
    out[...] = back(me, grad, (w0, w1), held)


def second_kernel(me, first, grad, w0, w1, keep, send, held):
    value = back(me, grad, (w0, w1), held)

    @pl.when(own_first(me))
    def _():
        keep[...] = first[...]
        send[...] = value.astype(BF16)

    @pl.when(jnp.logical_not(own_first(me)))
    def _():
        keep[...] = value
        send[...] = first[...].astype(BF16)


def call(kernel, outs, scratch, flops, *args):
    vmem = pl.BlockSpec(memory_space=pltpu.VMEM)
    return pl.pallas_call(
        kernel,
        out_shape=outs,
        in_specs=[pl.BlockSpec(memory_space=pltpu.SMEM)] + [vmem] * (len(args) - 1),
        out_specs=[vmem] * len(outs),
        scratch_shapes=scratch,
        compiler_params=pltpu.CompilerParams(vmem_limit_bytes=12 * 1024 * 1024),
        cost_estimate=pl.CostEstimate(
            flops=flops, bytes_accessed=3 * 1024 * 1024, transcendentals=0
        ),
    )(*args)


def shape(rows, columns, dtype):
    return jax.ShapeDtypeStruct((rows, columns), dtype)


def shards(acts, weight, cotangent):
    row, col = lax.axis_index("row"), lax.axis_index("col")
    me = jnp.stack([row, col]).astype(jnp.int32)
    upper = ((row >> 1) & 1) == 1
    odd = (col & 1) == 1
    part, depth = acts.shape
    width = weight.shape[1]
    tokens = part * COLS
    flops = tokens * depth * width

    pair = jnp.concatenate([acts, swap(acts, "col", 16)])
    partner = swap(weight, "col", 1)
    line = lax.all_gather(pair, "col", axis=0, tiled=True, axis_index_groups=Z_GROUPS)
    across = swap(line, "col", 2)

    size = tokens // 2
    held = [pltpu.VMEM((tokens // 4, depth), BF16)]
    (early,) = call(
        early_kernel, [shape(size, width, F32)], held, flops, me, line, weight, partner
    )

    late, send = call(
        send_kernel,
        [shape(size, width, F32), shape(size, width, BF16)],
        held, flops, me, early, across, weight, partner,
    )

    (mine,) = call(
        keep_kernel,
        [shape(size, width, BF16)],
        [], size * width, me, early, late, swap(send, "row", 1),
    )
    size = tokens // 8
    got = spread(mine, "row", Y_GROUPS)
    mine = total([got[y * size : (y + 1) * size] for y in range(4)])
    (sent,) = call(
        hold_kernel, [shape(size, width, BF16)], [], 0, me, mine.astype(BF16)
    )
    pre = sent.astype(F32) + swap(sent, "row", 2).astype(F32)

    other = swap(cotangent, "row", 2)
    mine, theirs = call(
        pick_kernel, [shape(2 * part, width, BF16)] * 2, [], 0, me, cotangent, other, sent
    )
    (both,) = call(
        stack_kernel, [shape(4 * part, width, BF16)], [], 0, me, mine, swap(theirs, "col", 1)
    )

    size = tokens // 16
    value = gelu_value(jnp.where(upper, pre[size:], pre[:size])).astype(BF16)
    grad = (both.astype(F32) * gelu_slope(pre)).astype(BF16)
    mine, fetched = value[:part], swap(value[part:], "col", 1)
    output = jnp.concatenate([jnp.where(odd, fetched, mine), jnp.where(odd, mine, fetched)])

    g0 = lax.all_gather(grad, "row", axis=0, tiled=True, axis_index_groups=Y_GROUPS)
    g1 = swap(g0, "row", 1)

    size = tokens // 2
    (near,) = call(order_kernel, [shape(size, depth, BF16)], [], 0, me, line, across, sent)
    far = swap(near, "col", 1)

    size = tokens // 4
    held = [pltpu.VMEM((2, size, width), BF16)]
    (first,) = call(
        first_kernel,
        [shape(size, depth, F32)],
        held, flops, me, g0, far, weight, partner,
    )
    keep, send = call(
        second_kernel,
        [shape(size, depth, F32), shape(size, depth, BF16)],
        held, flops, me, first, g1, weight, partner,
    )

    mine = total([keep, swap(send, "col", 2)]).astype(BF16)
    size = tokens // 16
    got = spread(mine, "col", Z_GROUPS)
    mine = total([got[k * size : (k + 1) * size] for k in range(4)])
    acts_grad = total([mine[:part], swap(mine[part:].astype(BF16), "col", 16)]).astype(BF16)

    split = [g.reshape(8, 2, part, width) for g in (g0, g1)]
    own = [g[:, 0].reshape(-1, width) for g in split]
    others = [swap(split[0][:, 1].reshape(-1, width), "col", 1)]
    others += [swap(others[0], "row", 1)]
    weight_sum = lax.dot_general(
        jnp.concatenate([near, far]),
        jnp.concatenate(own + others),
        (((0,), (0,)), ((), ())),
        preferred_element_type=F32,
    )
    weight_grad = (weight_sum * tokens ** (-0.5)).astype(BF16)
    return (output, acts_grad, weight_grad)


def solution(mesh):
    in_specs = (P("col", "row"), P("row", "col"), P("row", "col"))
    out_specs = (P("row", "col"), P("col", "row"), P("row", "col"))
    return jax.shard_map(shards, mesh=mesh, in_specs=in_specs, out_specs=out_specs, check_vma=False)
```

```python
import functools
import math

import jax
import jax.numpy as jnp
from jax import lax
from jax.experimental import pallas as pl
from jax.experimental.pallas import tpu as pltpu
from jax.sharding import PartitionSpec as P

ROWS, COLS = 16, 32
F32, BF16 = jnp.float32, jnp.bfloat16
Y_GROUPS = [[y * 4 + low for y in range(4)] for low in range(4)]
Z_GROUPS = [[(h * 4 + z) * 4 + x for z in range(4)] for h in range(2) for x in range(4)]


def gelu_value(pre):
    return 0.5 * pre * (1.0 + lax.erf(pre / math.sqrt(2.0)))


def gelu_slope(pre):
    return 0.5 * (1.0 + lax.erf(pre / math.sqrt(2.0))) + pre * jnp.exp(
        -0.5 * pre * pre
    ) / math.sqrt(2.0 * math.pi)


def swap(value, axis, mask):
    size = ROWS if axis == "row" else COLS
    return lax.ppermute(value, axis, [(i, i ^ mask) for i in range(size)])


def spread(value, axis, groups):
    return lax.all_to_all(
        value, axis, split_axis=0, concat_axis=0, axis_index_groups=groups, tiled=True
    )


def total(parts):
    parts = [p.astype(F32) for p in parts]
    return functools.reduce(lambda a, b: a + b, parts)


def line_place(z, me_col):
    return (z & 3) * 2 + ((z >> 2) ^ (me_col >> 4))


def own_first(me):
    return ((me[0] ^ (me[1] >> 1)) & 1) == 0


def products(me, piece, weights, held, out):
    part = held.shape[0] // 8
    for z in range(8):
        src = pl.multiple_of(line_place(z, me[1]) * part, part)
        held[pl.ds(z * part, part), :] = piece[pl.ds(src, part), :]
    for block, w in enumerate(weights):
        value = jnp.dot(held[...], w[...], preferred_element_type=F32)
        for z in range(8):
            out[pl.ds((z * 2 + block) * part, part), :] = value[z * part : (z + 1) * part]


def early_kernel(me, piece, w0, w1, out, held):
    products(me, piece, (w0, w1), held, out)


def send_kernel(me, early, piece, w0, w1, late, send, held):
    products(me, piece, (w0, w1), held, late)

    @pl.when(own_first(me))
    def _():
        send[...] = late[...].astype(BF16)

    @pl.when(jnp.logical_not(own_first(me)))
    def _():
        send[...] = early[...].astype(BF16)


def keep_kernel(me, early, late, got, out):
    @pl.when(own_first(me))
    def _():
        out[...] = (early[...] + got[...].astype(F32)).astype(BF16)

    @pl.when(jnp.logical_not(own_first(me)))
    def _():
        out[...] = (late[...] + got[...].astype(F32)).astype(BF16)


def four_kernel(me, got, out):
    size = out.shape[0]
    value = got[:size].astype(F32)
    for y in range(1, 4):
        value += got[y * size : (y + 1) * size].astype(F32)
    out[...] = value.astype(BF16)


def pick_kernel(me, own, other, _, mine, theirs):
    part = own.shape[0] // 2
    upper, odd = (me[0] >> 1) & 1, me[1] & 1
    for piece, z in ((own, upper), (other, 1 - upper)):
        to = pl.ds(pl.multiple_of(z * part, part), part)
        mine[to, :] = piece[pl.ds(pl.multiple_of(odd * part, part), part), :]
        theirs[to, :] = piece[pl.ds(pl.multiple_of((1 - odd) * part, part), part), :]


def stack_kernel(me, mine, got, out):
    part = mine.shape[0] // 2
    for z in range(2):
        out[2 * z * part : (2 * z + 1) * part] = mine[z * part : (z + 1) * part]
        out[(2 * z + 1) * part : (2 * z + 2) * part] = got[z * part : (z + 1) * part]


def order_kernel(me, line, across, _, out):
    half = line.shape[0]
    part = half // 8
    swapped = (me[0] ^ (me[1] >> 1)) & 1
    for s, piece in enumerate((line, across)):
        for z in range(8):
            src = pl.multiple_of(line_place(z, me[1]) * part, part)
            to = pl.multiple_of((s ^ swapped) * half + z * part, part)
            out[pl.ds(to, part), :] = piece[pl.ds(src, part), :]


def back(me, grad, weights, held):
    size = held.shape[1]
    part = size // 8
    for z in range(8):
        to = pl.multiple_of(line_place(z, me[1]) * part, part)
        for block in range(2):
            held[block, pl.ds(to, part), :] = grad[pl.ds((z * 2 + block) * part, part), :]
    values = [
        lax.dot_general(
            held[block], w[...], (((1,), (1,)), ((), ())), preferred_element_type=F32
        )
        for block, w in enumerate(weights)
    ]
    return values[0] + values[1]


def first_kernel(me, grad, _, w0, w1, out, theirs, held):
    part = theirs.shape[0] // 8
    for z in range(8):
        theirs[z * part : (z + 1) * part] = grad[(2 * z + 1) * part : (2 * z + 2) * part]
    out[...] = back(me, grad, (w0, w1), held)


def second_kernel(me, first, grad, w0, w1, keep, send, held):
    value = back(me, grad, (w0, w1), held)

    @pl.when(own_first(me))
    def _():
        keep[...] = first[...]
        send[...] = value.astype(BF16)

    @pl.when(jnp.logical_not(own_first(me)))
    def _():
        keep[...] = value
        send[...] = first[...].astype(BF16)


def call(kernel, outs, scratch, flops, *args):
    vmem = pl.BlockSpec(memory_space=pltpu.VMEM)
    return pl.pallas_call(
        kernel,
        out_shape=outs,
        in_specs=[pl.BlockSpec(memory_space=pltpu.SMEM)] + [vmem] * (len(args) - 1),
        out_specs=[vmem] * len(outs),
        scratch_shapes=scratch,
        compiler_params=pltpu.CompilerParams(vmem_limit_bytes=12 * 1024 * 1024),
        cost_estimate=pl.CostEstimate(
            flops=flops, bytes_accessed=3 * 1024 * 1024, transcendentals=0
        ),
    )(*args)


def shape(rows, columns, dtype):
    return jax.ShapeDtypeStruct((rows, columns), dtype)


def shards(acts, weight, cotangent):
    row, col = lax.axis_index("row"), lax.axis_index("col")
    me = jnp.stack([row, col]).astype(jnp.int32)
    upper = ((row >> 1) & 1) == 1
    odd = (col & 1) == 1
    part, depth = acts.shape
    width = weight.shape[1]
    tokens = part * COLS
    flops = tokens * depth * width

    pair = jnp.concatenate([acts, swap(acts, "col", 16)])
    partner = swap(weight, "col", 1)
    line = lax.all_gather(pair, "col", axis=0, tiled=True, axis_index_groups=Z_GROUPS)
    across = swap(line, "col", 2)

    size = tokens // 2
    held = [pltpu.VMEM((tokens // 4, depth), BF16)]
    (early,) = call(
        early_kernel, [shape(size, width, F32)], held, flops, me, line, weight, partner
    )

    late, send = call(
        send_kernel,
        [shape(size, width, F32), shape(size, width, BF16)],
        held, flops, me, early, across, weight, partner,
    )

    (mine,) = call(
        keep_kernel,
        [shape(size, width, BF16)],
        [], size * width, me, early, late, swap(send, "row", 1),
    )
    size = tokens // 8
    (sent,) = call(
        four_kernel, [shape(size, width, BF16)], [], 0, me, spread(mine, "row", Y_GROUPS)
    )
    pre = sent.astype(F32) + swap(sent, "row", 2).astype(F32)

    other = swap(cotangent, "row", 2)
    mine, theirs = call(
        pick_kernel, [shape(2 * part, width, BF16)] * 2, [], 0, me, cotangent, other, sent
    )
    (both,) = call(
        stack_kernel, [shape(4 * part, width, BF16)], [], 0, me, mine, swap(theirs, "col", 1)
    )

    size = tokens // 16
    value = gelu_value(jnp.where(upper, pre[size:], pre[:size])).astype(BF16)
    grad = (both.astype(F32) * gelu_slope(pre)).astype(BF16)
    mine, fetched = value[:part], swap(value[part:], "col", 1)
    output = jnp.concatenate([jnp.where(odd, fetched, mine), jnp.where(odd, mine, fetched)])

    g0 = lax.all_gather(grad, "row", axis=0, tiled=True, axis_index_groups=Y_GROUPS)
    g1 = swap(g0, "row", 1)

    size = tokens // 2
    (near,) = call(order_kernel, [shape(size, depth, BF16)], [], 0, me, line, across, sent)
    far = swap(near, "col", 1)

    size = tokens // 4
    held = [pltpu.VMEM((2, size, width), BF16)]
    first, theirs = call(
        first_kernel,
        [shape(size, depth, F32), shape(size, width, BF16)],
        held, flops, me, g0, far, weight, partner,
    )
    keep, send = call(
        second_kernel,
        [shape(size, depth, F32), shape(size, depth, BF16)],
        held, flops, me, first, g1, weight, partner,
    )

    mine = total([keep, swap(send, "col", 2)]).astype(BF16)
    size = tokens // 16
    got = spread(mine, "col", Z_GROUPS)
    mine = total([got[k * size : (k + 1) * size] for k in range(4)])
    acts_grad = total([mine[:part], swap(mine[part:].astype(BF16), "col", 16)]).astype(BF16)

    split = [g.reshape(8, 2, part, width) for g in (g0, g1)]
    own = [g[:, 0].reshape(-1, width) for g in split]
    others = [swap(theirs, "col", 1)]
    others += [swap(others[0], "row", 1)]
    weight_sum = lax.dot_general(
        jnp.concatenate([near, far]),
        jnp.concatenate(own + others),
        (((0,), (0,)), ((), ())),
        preferred_element_type=F32,
    )
    weight_grad = (weight_sum * tokens ** (-0.5)).astype(BF16)
    return (output, acts_grad, weight_grad)


def solution(mesh):
    in_specs = (P("col", "row"), P("row", "col"), P("row", "col"))
    out_specs = (P("row", "col"), P("col", "row"), P("row", "col"))
    return jax.shard_map(shards, mesh=mesh, in_specs=in_specs, out_specs=out_specs, check_vma=False)
```

```python
import functools
import math

import jax
import jax.numpy as jnp
from jax import lax
from jax.experimental import pallas as pl
from jax.experimental.pallas import tpu as pltpu
from jax.sharding import PartitionSpec as P

ROWS, COLS = 16, 32
F32, BF16 = jnp.float32, jnp.bfloat16
Y_GROUPS = [[y * 4 + low for y in range(4)] for low in range(4)]
Z_GROUPS = [[(h * 4 + z) * 4 + x for z in range(4)] for h in range(2) for x in range(4)]


def gelu_value(pre):
    return 0.5 * pre * (1.0 + lax.erf(pre / math.sqrt(2.0)))


def gelu_slope(pre):
    return 0.5 * (1.0 + lax.erf(pre / math.sqrt(2.0))) + pre * jnp.exp(
        -0.5 * pre * pre
    ) / math.sqrt(2.0 * math.pi)


def swap(value, axis, mask):
    size = ROWS if axis == "row" else COLS
    return lax.ppermute(value, axis, [(i, i ^ mask) for i in range(size)])


def spread(value, axis, groups):
    return lax.all_to_all(
        value, axis, split_axis=0, concat_axis=0, axis_index_groups=groups, tiled=True
    )


def total(parts):
    parts = [p.astype(F32) for p in parts]
    return functools.reduce(lambda a, b: a + b, parts)


def line_place(z, me_col):
    return (z & 3) * 2 + ((z >> 2) ^ (me_col >> 4))


def gather_place(z, x, me_col):
    return (z & 3) * 4 + x * 2 + ((z >> 2) ^ (me_col >> 4))


def own_first(me):
    return ((me[0] ^ (me[1] >> 1)) & 1) == 0


def products(me, line, x, weights, held, out):
    part = held.shape[0] // 8
    for z in range(8):
        src = pl.multiple_of(gather_place(z, x, me[1]) * part, part)
        held[pl.ds(z * part, part), :] = line[pl.ds(src, part), :]
    for block, w in enumerate(weights):
        value = jnp.dot(held[...], w[...], preferred_element_type=F32)
        for z in range(8):
            out[pl.ds((z * 2 + block) * part, part), :] = value[z * part : (z + 1) * part]


def up_kernel(me, line, w0, w1, early, late, send, held):
    products(me, line, 0, (w0, w1), held, early)
    products(me, line, 1, (w0, w1), held, late)

    @pl.when(own_first(me))
    def _():
        send[...] = late[...].astype(BF16)

    @pl.when(jnp.logical_not(own_first(me)))
    def _():
        send[...] = early[...].astype(BF16)


def keep_kernel(me, early, late, got, out):
    @pl.when(own_first(me))
    def _():
        out[...] = (early[...] + got[...].astype(F32)).astype(BF16)

    @pl.when(jnp.logical_not(own_first(me)))
    def _():
        out[...] = (late[...] + got[...].astype(F32)).astype(BF16)


def four_kernel(me, got, out):
    size = out.shape[0]
    value = got[:size].astype(F32)
    for y in range(1, 4):
        value += got[y * size : (y + 1) * size].astype(F32)
    out[...] = value.astype(BF16)


def pick_kernel(me, own, other, _, mine, theirs):
    part = own.shape[0] // 2
    upper, odd = (me[0] >> 1) & 1, me[1] & 1
    for piece, z in ((own, upper), (other, 1 - upper)):
        to = pl.ds(pl.multiple_of(z * part, part), part)
        mine[to, :] = piece[pl.ds(pl.multiple_of(odd * part, part), part), :]
        theirs[to, :] = piece[pl.ds(pl.multiple_of((1 - odd) * part, part), part), :]


def stack_kernel(me, mine, got, out):
    part = mine.shape[0] // 2
    for z in range(2):
        out[2 * z * part : (2 * z + 1) * part] = mine[z * part : (z + 1) * part]
        out[(2 * z + 1) * part : (2 * z + 2) * part] = got[z * part : (z + 1) * part]


def order_kernel(me, line, _, out):
    half = line.shape[0] // 2
    part = half // 8
    swapped = (me[0] ^ (me[1] >> 1)) & 1
    for s in range(2):
        for z in range(8):
            src = pl.multiple_of(gather_place(z, s, me[1]) * part, part)
            to = pl.multiple_of((s ^ swapped) * half + z * part, part)
            out[pl.ds(to, part), :] = line[pl.ds(src, part), :]


def back(me, grad, weights, held):
    size = held.shape[1]
    part = size // 8
    for z in range(8):
        to = pl.multiple_of(line_place(z, me[1]) * part, part)
        for block in range(2):
            held[block, pl.ds(to, part), :] = grad[pl.ds((z * 2 + block) * part, part), :]
    values = [
        lax.dot_general(
            held[block], w[...], (((1,), (1,)), ((), ())), preferred_element_type=F32
        )
        for block, w in enumerate(weights)
    ]
    return values[0] + values[1]


def first_kernel(me, grad, _, w0, w1, out, theirs, held):
    part = theirs.shape[0] // 8
    for z in range(8):
        theirs[z * part : (z + 1) * part] = grad[(2 * z + 1) * part : (2 * z + 2) * part]
    out[...] = back(me, grad, (w0, w1), held)


def second_kernel(me, first, grad, w0, w1, keep, send, held):
    value = back(me, grad, (w0, w1), held)

    @pl.when(own_first(me))
    def _():
        keep[...] = first[...]
        send[...] = value.astype(BF16)

    @pl.when(jnp.logical_not(own_first(me)))
    def _():
        keep[...] = value
        send[...] = first[...].astype(BF16)


def call(kernel, outs, scratch, flops, *args):
    vmem = pl.BlockSpec(memory_space=pltpu.VMEM)
    return pl.pallas_call(
        kernel,
        out_shape=outs,
        in_specs=[pl.BlockSpec(memory_space=pltpu.SMEM)] + [vmem] * (len(args) - 1),
        out_specs=[vmem] * len(outs),
        scratch_shapes=scratch,
        compiler_params=pltpu.CompilerParams(vmem_limit_bytes=12 * 1024 * 1024),
        cost_estimate=pl.CostEstimate(
            flops=flops, bytes_accessed=3 * 1024 * 1024, transcendentals=0
        ),
    )(*args)


def shape(rows, columns, dtype):
    return jax.ShapeDtypeStruct((rows, columns), dtype)


def shards(acts, weight, cotangent):
    row, col = lax.axis_index("row"), lax.axis_index("col")
    me = jnp.stack([row, col]).astype(jnp.int32)
    upper = ((row >> 1) & 1) == 1
    odd = (col & 1) == 1
    part, depth = acts.shape
    width = weight.shape[1]
    tokens = part * COLS
    flops = tokens * depth * width

    pair = jnp.concatenate([acts] + [swap(acts, "col", mask) for mask in (16, 2, 18)])
    partner = swap(weight, "col", 1)
    line = lax.all_gather(pair, "col", axis=0, tiled=True, axis_index_groups=Z_GROUPS)

    size = tokens // 2
    held = [pltpu.VMEM((tokens // 4, depth), BF16)]
    early, late, send = call(
        up_kernel,
        [shape(size, width, F32)] * 2 + [shape(size, width, BF16)],
        held, 2 * flops, me, line, weight, partner,
    )

    (mine,) = call(
        keep_kernel,
        [shape(size, width, BF16)],
        [], size * width, me, early, late, swap(send, "row", 1),
    )
    size = tokens // 8
    (sent,) = call(
        four_kernel, [shape(size, width, BF16)], [], 0, me, spread(mine, "row", Y_GROUPS)
    )
    pre = sent.astype(F32) + swap(sent, "row", 2).astype(F32)

    other = swap(cotangent, "row", 2)
    mine, theirs = call(
        pick_kernel, [shape(2 * part, width, BF16)] * 2, [], 0, me, cotangent, other, sent
    )
    (both,) = call(
        stack_kernel, [shape(4 * part, width, BF16)], [], 0, me, mine, swap(theirs, "col", 1)
    )

    size = tokens // 16
    value = gelu_value(jnp.where(upper, pre[size:], pre[:size])).astype(BF16)
    grad = (both.astype(F32) * gelu_slope(pre)).astype(BF16)
    mine, fetched = value[:part], swap(value[part:], "col", 1)
    output = jnp.concatenate([jnp.where(odd, fetched, mine), jnp.where(odd, mine, fetched)])

    g0 = lax.all_gather(grad, "row", axis=0, tiled=True, axis_index_groups=Y_GROUPS)
    g1 = swap(g0, "row", 1)

    size = tokens // 2
    (near,) = call(order_kernel, [shape(size, depth, BF16)], [], 0, me, line, sent)
    far = swap(near, "col", 1)

    size = tokens // 4
    held = [pltpu.VMEM((2, size, width), BF16)]
    first, theirs = call(
        first_kernel,
        [shape(size, depth, F32), shape(size, width, BF16)],
        held, flops, me, g0, far, weight, partner,
    )
    keep, send = call(
        second_kernel,
        [shape(size, depth, F32), shape(size, depth, BF16)],
        held, flops, me, first, g1, weight, partner,
    )

    mine = total([keep, swap(send, "col", 2)]).astype(BF16)
    size = tokens // 16
    got = spread(mine, "col", Z_GROUPS)
    mine = total([got[k * size : (k + 1) * size] for k in range(4)])
    acts_grad = total([mine[:part], swap(mine[part:].astype(BF16), "col", 16)]).astype(BF16)

    split = [g.reshape(8, 2, part, width) for g in (g0, g1)]
    own = [g[:, 0].reshape(-1, width) for g in split]
    others = [swap(theirs, "col", 1)]
    others += [swap(others[0], "row", 1)]
    weight_sum = lax.dot_general(
        jnp.concatenate([near, far]),
        jnp.concatenate(own + others),
        (((0,), (0,)), ((), ())),
        preferred_element_type=F32,
    )
    weight_grad = (weight_sum * tokens ** (-0.5)).astype(BF16)
    return (output, acts_grad, weight_grad)


def solution(mesh):
    in_specs = (P("col", "row"), P("row", "col"), P("row", "col"))
    out_specs = (P("row", "col"), P("col", "row"), P("row", "col"))
    return jax.shard_map(shards, mesh=mesh, in_specs=in_specs, out_specs=out_specs, check_vma=False)
```

```python
import functools
import math

import jax
import jax.numpy as jnp
from jax import lax
from jax.experimental import pallas as pl
from jax.experimental.pallas import tpu as pltpu
from jax.sharding import PartitionSpec as P

ROWS, COLS = 16, 32
F32, BF16 = jnp.float32, jnp.bfloat16
Y_GROUPS = [[y * 4 + low for y in range(4)] for low in range(4)]
Z_GROUPS = [[(h * 4 + z) * 4 + x for z in range(4)] for h in range(2) for x in range(4)]


def gelu_value(pre):
    return 0.5 * pre * (1.0 + lax.erf(pre / math.sqrt(2.0)))


def gelu_slope(pre):
    return 0.5 * (1.0 + lax.erf(pre / math.sqrt(2.0))) + pre * jnp.exp(
        -0.5 * pre * pre
    ) / math.sqrt(2.0 * math.pi)


def swap(value, axis, mask):
    size = ROWS if axis == "row" else COLS
    return lax.ppermute(value, axis, [(i, i ^ mask) for i in range(size)])


def spread(value, axis, groups):
    return lax.all_to_all(
        value, axis, split_axis=0, concat_axis=0, axis_index_groups=groups, tiled=True
    )


def total(parts):
    parts = [p.astype(F32) for p in parts]
    return functools.reduce(lambda a, b: a + b, parts)


def line_place(z, me_col):
    return (z & 3) * 2 + ((z >> 2) ^ (me_col >> 4))


def gather_place(z, x, me_col):
    return (z & 3) * 4 + x * 2 + ((z >> 2) ^ (me_col >> 4))


def own_first(me):
    return ((me[0] ^ (me[1] >> 1)) & 1) == 0


def products(me, line, x, weights, held, out):
    part = held.shape[0] // 8
    for z in range(8):
        src = pl.multiple_of(gather_place(z, x, me[1]) * part, part)
        held[pl.ds(z * part, part), :] = line[pl.ds(src, part), :]
    for block, w in enumerate(weights):
        value = jnp.dot(held[...], w[...], preferred_element_type=F32)
        for z in range(8):
            out[pl.ds((z * 2 + block) * part, part), :] = value[z * part : (z + 1) * part]


def up_kernel(me, line, w0, w1, early, late, send, held):
    products(me, line, 0, (w0, w1), held, early)
    products(me, line, 1, (w0, w1), held, late)

    @pl.when(own_first(me))
    def _():
        send[...] = late[...].astype(BF16)

    @pl.when(jnp.logical_not(own_first(me)))
    def _():
        send[...] = early[...].astype(BF16)


def keep_kernel(me, early, late, got, out):
    @pl.when(own_first(me))
    def _():
        out[...] = (early[...] + got[...].astype(F32)).astype(BF16)

    @pl.when(jnp.logical_not(own_first(me)))
    def _():
        out[...] = (late[...] + got[...].astype(F32)).astype(BF16)


def after_kernel(me, value, _, __, out):
    out[...] = value[...]


def four_kernel(me, got, out):
    size = out.shape[0]
    value = got[:size].astype(F32)
    for y in range(1, 4):
        value += got[y * size : (y + 1) * size].astype(F32)
    out[...] = value.astype(BF16)


def pick_kernel(me, own, other, _, mine, theirs):
    part = own.shape[0] // 2
    upper, odd = (me[0] >> 1) & 1, me[1] & 1
    for piece, z in ((own, upper), (other, 1 - upper)):
        to = pl.ds(pl.multiple_of(z * part, part), part)
        mine[to, :] = piece[pl.ds(pl.multiple_of(odd * part, part), part), :]
        theirs[to, :] = piece[pl.ds(pl.multiple_of((1 - odd) * part, part), part), :]


def stack_kernel(me, mine, got, out):
    part = mine.shape[0] // 2
    for z in range(2):
        out[2 * z * part : (2 * z + 1) * part] = mine[z * part : (z + 1) * part]
        out[(2 * z + 1) * part : (2 * z + 2) * part] = got[z * part : (z + 1) * part]


def order_kernel(me, line, _, out):
    half = line.shape[0] // 2
    part = half // 8
    swapped = (me[0] ^ (me[1] >> 1)) & 1
    for s in range(2):
        for z in range(8):
            src = pl.multiple_of(gather_place(z, s, me[1]) * part, part)
            to = pl.multiple_of((s ^ swapped) * half + z * part, part)
            out[pl.ds(to, part), :] = line[pl.ds(src, part), :]


def back(me, grad, weights, held):
    size = held.shape[1]
    part = size // 8
    for z in range(8):
        to = pl.multiple_of(line_place(z, me[1]) * part, part)
        for block in range(2):
            held[block, pl.ds(to, part), :] = grad[pl.ds((z * 2 + block) * part, part), :]
    values = [
        lax.dot_general(
            held[block], w[...], (((1,), (1,)), ((), ())), preferred_element_type=F32
        )
        for block, w in enumerate(weights)
    ]
    return values[0] + values[1]


def first_kernel(me, grad, _, w0, w1, out, theirs, held):
    part = theirs.shape[0] // 8
    for z in range(8):
        theirs[z * part : (z + 1) * part] = grad[(2 * z + 1) * part : (2 * z + 2) * part]
    out[...] = back(me, grad, (w0, w1), held)


def second_kernel(me, first, grad, w0, w1, keep, send, held):
    value = back(me, grad, (w0, w1), held)

    @pl.when(own_first(me))
    def _():
        keep[...] = first[...]
        send[...] = value.astype(BF16)

    @pl.when(jnp.logical_not(own_first(me)))
    def _():
        keep[...] = value
        send[...] = first[...].astype(BF16)


def call(kernel, outs, scratch, flops, *args):
    vmem = pl.BlockSpec(memory_space=pltpu.VMEM)
    return pl.pallas_call(
        kernel,
        out_shape=outs,
        in_specs=[pl.BlockSpec(memory_space=pltpu.SMEM)] + [vmem] * (len(args) - 1),
        out_specs=[vmem] * len(outs),
        scratch_shapes=scratch,
        compiler_params=pltpu.CompilerParams(vmem_limit_bytes=12 * 1024 * 1024),
        cost_estimate=pl.CostEstimate(
            flops=flops, bytes_accessed=3 * 1024 * 1024, transcendentals=0
        ),
    )(*args)


def shape(rows, columns, dtype):
    return jax.ShapeDtypeStruct((rows, columns), dtype)


def shards(acts, weight, cotangent):
    row, col = lax.axis_index("row"), lax.axis_index("col")
    me = jnp.stack([row, col]).astype(jnp.int32)
    upper = ((row >> 1) & 1) == 1
    odd = (col & 1) == 1
    part, depth = acts.shape
    width = weight.shape[1]
    tokens = part * COLS
    flops = tokens * depth * width

    blocks = [swap(acts, "col", mask) for mask in (16, 2, 18)]
    pair = jnp.concatenate([acts] + blocks)
    (ready,) = call(after_kernel, [shape(depth, width, BF16)], [], 0, me, weight, *blocks[1:])
    partner = swap(ready, "col", 1)
    line = lax.all_gather(pair, "col", axis=0, tiled=True, axis_index_groups=Z_GROUPS)

    size = tokens // 2
    held = [pltpu.VMEM((tokens // 4, depth), BF16)]
    early, late, send = call(
        up_kernel,
        [shape(size, width, F32)] * 2 + [shape(size, width, BF16)],
        held, 2 * flops, me, line, weight, partner,
    )

    (mine,) = call(
        keep_kernel,
        [shape(size, width, BF16)],
        [], size * width, me, early, late, swap(send, "row", 1),
    )
    size = tokens // 8
    (sent,) = call(
        four_kernel, [shape(size, width, BF16)], [], 0, me, spread(mine, "row", Y_GROUPS)
    )
    pre = sent.astype(F32) + swap(sent, "row", 2).astype(F32)

    other = swap(cotangent, "row", 2)
    mine, theirs = call(
        pick_kernel, [shape(2 * part, width, BF16)] * 2, [], 0, me, cotangent, other, sent
    )
    (both,) = call(
        stack_kernel, [shape(4 * part, width, BF16)], [], 0, me, mine, swap(theirs, "col", 1)
    )

    size = tokens // 16
    value = gelu_value(jnp.where(upper, pre[size:], pre[:size])).astype(BF16)
    grad = (both.astype(F32) * gelu_slope(pre)).astype(BF16)
    mine, fetched = value[:part], swap(value[part:], "col", 1)
    output = jnp.concatenate([jnp.where(odd, fetched, mine), jnp.where(odd, mine, fetched)])

    g0 = lax.all_gather(grad, "row", axis=0, tiled=True, axis_index_groups=Y_GROUPS)
    g1 = swap(g0, "row", 1)

    size = tokens // 2
    (near,) = call(order_kernel, [shape(size, depth, BF16)], [], 0, me, line, sent)
    far = swap(near, "col", 1)

    size = tokens // 4
    held = [pltpu.VMEM((2, size, width), BF16)]
    first, theirs = call(
        first_kernel,
        [shape(size, depth, F32), shape(size, width, BF16)],
        held, flops, me, g0, far, weight, partner,
    )
    keep, send = call(
        second_kernel,
        [shape(size, depth, F32), shape(size, depth, BF16)],
        held, flops, me, first, g1, weight, partner,
    )

    mine = total([keep, swap(send, "col", 2)]).astype(BF16)
    size = tokens // 16
    got = spread(mine, "col", Z_GROUPS)
    mine = total([got[k * size : (k + 1) * size] for k in range(4)])
    acts_grad = total([mine[:part], swap(mine[part:].astype(BF16), "col", 16)]).astype(BF16)

    split = [g.reshape(8, 2, part, width) for g in (g0, g1)]
    own = [g[:, 0].reshape(-1, width) for g in split]
    others = [swap(theirs, "col", 1)]
    others += [swap(others[0], "row", 1)]
    weight_sum = lax.dot_general(
        jnp.concatenate([near, far]),
        jnp.concatenate(own + others),
        (((0,), (0,)), ((), ())),
        preferred_element_type=F32,
    )
    weight_grad = (weight_sum * tokens ** (-0.5)).astype(BF16)
    return (output, acts_grad, weight_grad)


def solution(mesh):
    in_specs = (P("col", "row"), P("row", "col"), P("row", "col"))
    out_specs = (P("row", "col"), P("col", "row"), P("row", "col"))
    return jax.shard_map(shards, mesh=mesh, in_specs=in_specs, out_specs=out_specs, check_vma=False)
```
